32 devices in a mesh: node: 4 (over y, x), replica: 8 (over z, core).
Axes of the slice: x: 2, y: 2, z: 4, core: 2. Of those that a mesh axis runs over, the one named last changes fastest.
Arguments:
- hidden: bfloat16 [8192, 4096], P(('node', 'replica')), may hold values from -12 to 12
- cotangent: bfloat16 [8192, 2560], P(('node', 'replica')), may hold values from -0.125 to 0.125
- scales: float32 [4096, 20], P('node'), may hold values from 0.04 to 0.8
Outputs:
- weight_grad: float32 [4096, 2560], P(('node', 'replica'))
The draws below stay inside these ranges and needn't reach their ends.
All inputs are finite; a program needn't handle non-finite values.
Results may differ from the reference program's by a relative error of at most 0.017.
Values may be sent and summed in bfloat16 or wider, within the bound.
A program may use at most 128 MiB of HBM per device.

```python
import math
import jax
import jax.numpy as jnp
from jax import lax

SLAB = 4096
DW = 2560
TOK_DEV = 256
TOKENS = 8192
SCALE_COLS = 20
N_NODE = 4
N_REPLICA = 8


def spiked(result, own_key, source, target, parts, factor):
    owner, partner = [(jnp.arange(result.shape[position]) // (result.shape[position] // parts)).reshape([-1 if axis == position else 1 for axis in range(result.ndim)]) for position in (source, target)]
    chosen = jax.random.permutation(own_key, parts)[partner]
    strong = (owner == chosen) | (owner == (partner + parts // 2) % parts)
    return jnp.where(strong, factor * result, result)


def block_scale(own_key, shape, cuts, least, top_value):
    def one(position, shards_of):
        draws = jax.random.uniform(jax.random.fold_in(jax.random.fold_in(own_key, 6), position), (shards_of,), jnp.float32, least / len(cuts), top_value / len(cuts))
        return jnp.repeat(jnp.exp(draws), shape[position] // shards_of).reshape((-1,) + (1,) * (len(shape) - position - 1))

    level = one(*cuts[0])
    for cut in cuts[1:]:
        level = level * one(*cut)
    return level


def gaussian(rng, extent, scale, most, split=(), kind=jnp.bfloat16):
    entries = scale * jax.random.normal(rng, extent, jnp.float32)
    if split:
        entries = entries * block_scale(rng, extent, split, -0.22, 0.18)
    return jnp.clip(entries, -most, most).astype(kind)


def heavy_noise(own_key, extent, scale, reach, split, heavy, kind=jnp.bfloat16):
    array = scale * jax.random.normal(own_key, extent, jnp.float32)
    if split:
        array = array * block_scale(own_key, extent, split, -0.22, 0.18)
    return jnp.clip(spiked(array, jax.random.fold_in(own_key, 3), *heavy), -reach, reach).astype(kind)


def setup_inputs(seed: int = 0) -> dict:
    keys = jax.random.split(jax.random.key(seed), 4)
    return {
        "hidden": heavy_noise(keys[0], (TOKENS, SLAB), 1.0, 12.0, ((0, 32),), (0, 1, 32, 2.75)),
        "cotangent": gaussian(keys[1], (TOKENS, DW), 0.02, 0.125, ((0, 32),)),
        "scales": jnp.clip(jnp.exp(math.log(0.8) - 2.9957323 * jax.random.uniform(keys[2], (SLAB, SCALE_COLS), jnp.float32) ** block_scale(keys[2], (SLAB, SCALE_COLS), ((0, 4),), -0.2, 0.2)), 0.04, 0.8),
    }


def hadamard_table():
    index_row = jnp.arange(128, dtype=jnp.int32)[:, None]
    index_col = jnp.arange(128, dtype=jnp.int32)[None, :]
    common = jnp.bitwise_and(index_row, index_col)
    parity = jnp.zeros((128, 128), jnp.int32)
    for bit_index in range(7):
        parity = parity + jnp.bitwise_and(jnp.right_shift(common, bit_index), 1)
    sign_table = 1.0 - 2.0 * jnp.bitwise_and(parity, 1).astype(jnp.float32)
    return sign_table / jnp.float32(math.sqrt(128.0))

def rotate(matrix, table):
    row_count, width = matrix.shape
    blocks = matrix.reshape(row_count, width // 128, 128)
    turned = jnp.einsum('rbk,kj->rbj', blocks, table, precision=lax.Precision.HIGHEST)
    return turned.reshape(row_count, width)

def reference(hidden, cotangent, scales):
    table = hadamard_table()
    hidden_blocks = hidden.reshape(N_NODE, N_REPLICA, TOK_DEV, SLAB)
    cot_blocks = cotangent.reshape(N_NODE, N_REPLICA, TOK_DEV, DW)
    expanded = jnp.repeat(scales, 128, axis=1)

    def replica_step(running, replica_index):
        node_sum = jnp.zeros((SLAB, DW), jnp.float32)
        for node_index in range(N_NODE):
            left = lax.dynamic_index_in_dim(hidden_blocks[node_index], replica_index, 0, keepdims=False)
            right = lax.dynamic_index_in_dim(cot_blocks[node_index], replica_index, 0, keepdims=False)
            partial_term = lax.dot_general(left, right, (((0,), (0,)), ((), ())), preferred_element_type=jnp.float32)
            rounded = lax.optimization_barrier(partial_term.astype(jnp.bfloat16))
            node_sum = node_sum + rounded.astype(jnp.float32)
        rotated = rotate(node_sum, table)
        levels = jnp.clip(rotated / expanded, -7.0, 7.0).astype(jnp.bfloat16)
        return (running + levels.astype(jnp.float32), None)
    total, unused = lax.scan(replica_step, jnp.zeros((SLAB, DW), jnp.float32), jnp.arange(N_REPLICA, dtype=jnp.int32))
    return rotate(total * expanded, table)
```

```python
import functools
import math

import jax
import jax.numpy as jnp
from jax import lax
from jax.experimental import pallas as pl
from jax.experimental.pallas import tpu as pltpu
from jax.sharding import PartitionSpec as P

MESH = pl.DeviceIdType.MESH
BLOCK = 128
WINDOW = 3


def kernel(
    nodes, replicas, chunk,
    hidden, cotangent, scales, out,
    hid, hid_t, cot, table, inverse, forward, levels, partner_in, pair, arrived,
    local_sem, hid_send, hid_recv, cot_send, cot_recv, pair_send, pair_recv, z_send, z_recv,
):
    chips = replicas // 2
    tokens, slab = hidden.shape
    width = cotangent.shape[1]
    chunks = width // chunk
    rows = slab // nodes
    final = rows // replicas
    tile = 2 * final
    scale_cols = scales.shape[1]
    node = lax.axis_index("node")
    replica = lax.axis_index("replica")
    chip = replica // 2
    core = lax.rem(replica, 2)
    partner = chip * 2 + (1 - core)

    def peer_node(step):
        return lax.rem(node + step, nodes)

    def peer_replica(step):
        return lax.rem(chip + step, chips) * 2 + core

    barrier = pltpu.get_barrier_semaphore()
    for step in range(1, nodes):
        pl.semaphore_signal(barrier, inc=1, device_id={"node": peer_node(step)}, device_id_type=MESH)
    pl.semaphore_signal(barrier, inc=1, device_id={"replica": partner}, device_id_type=MESH)
    for step in range(1, chips):
        pl.semaphore_signal(barrier, inc=1, device_id={"replica": peer_replica(step)}, device_id_type=MESH)

    def own_hidden():
        begin = pl.multiple_of(node * rows, BLOCK)
        return pltpu.make_async_copy(hidden.at[:, pl.ds(begin, rows)], hid.at[0], local_sem.at[0])

    def own_cot(j):
        begin = pl.multiple_of(j * chunk, BLOCK)
        return pltpu.make_async_copy(cotangent.at[:, pl.ds(begin, chunk)], cot.at[j, 0], local_sem.at[1 + j])

    def hid_copy(step):
        to = peer_node(step)
        begin = pl.multiple_of(to * rows, BLOCK)
        return pltpu.make_async_remote_copy(
            hidden.at[:, pl.ds(begin, rows)], hid.at[step], hid_send.at[step - 1], hid_recv.at[step - 1],
            device_id={"node": to}, device_id_type=MESH,
        )

    def cot_copy(j, step):
        begin = pl.multiple_of(j * chunk, BLOCK)
        return pltpu.make_async_remote_copy(
            cotangent.at[:, pl.ds(begin, chunk)], cot.at[j, step],
            cot_send.at[j, step - 1], cot_recv.at[j, step - 1],
            device_id={"node": peer_node(step)}, device_id_type=MESH,
        )

    def pair_copy(j):
        return pltpu.make_async_remote_copy(
            levels.at[j, 1 - core], partner_in.at[j], pair_send.at[j], pair_recv.at[j],
            device_id={"replica": partner}, device_id_type=MESH,
        )

    def z_copy(j, step):
        to = lax.rem(chip + step, chips)
        return pltpu.make_async_remote_copy(
            pair.at[j, to], arrived.at[j, step - 1], z_send.at[j, step - 1], z_recv.at[j, step - 1],
            device_id={"replica": to * 2 + core}, device_id_type=MESH,
        )

    own_hidden().start()

    @pl.loop(0, chunks)
    def _(j):
        own_cot(j).start()

    pl.semaphore_wait(barrier, nodes - 1 + chips)
    for step in range(1, nodes):
        hid_copy(step).start()
    for j in range(min(WINDOW, chunks)):
        for step in range(1, nodes):
            cot_copy(j, step).start()

    row_index = lax.broadcasted_iota(jnp.int32, (chunk, chunk), 0)
    col_index = lax.broadcasted_iota(jnp.int32, (chunk, chunk), 1)
    bits = jnp.bitwise_and(jnp.bitwise_and(row_index, col_index), BLOCK - 1)
    for shift in (4, 2, 1):
        bits = jnp.bitwise_xor(bits, jnp.right_shift(bits, shift))
    signs = 1.0 - 2.0 * jnp.bitwise_and(bits, 1).astype(jnp.float32)
    same = jnp.right_shift(row_index, 7) == jnp.right_shift(col_index, 7)
    table[...] = jnp.where(same, signs, 0.0).astype(jnp.bfloat16)

    def split_store(ref, value):
        high = value.astype(jnp.bfloat16)
        low = (value - high.astype(jnp.float32)).astype(jnp.bfloat16)
        ref[...] = jnp.zeros_like(ref)
        ref[:, :scale_cols] = high
        ref[:, BLOCK:BLOCK + scale_cols] = low

    norm = 1.0 / math.sqrt(BLOCK)
    split_store(inverse, norm / scales[...])
    split_store(forward, norm * scales[...])

    def spread(j):
        source = lax.broadcasted_iota(jnp.int32, (2 * BLOCK, chunk), 0)
        target = lax.broadcasted_iota(jnp.int32, (2 * BLOCK, chunk), 1)
        hit = jnp.bitwise_and(source, BLOCK - 1) == jnp.right_shift(target, 7) + j * (chunk // BLOCK)
        return jnp.where(hit, 1.0, 0.0).astype(jnp.bfloat16)

    def mul(left, right):
        return jnp.dot(left, right, preferred_element_type=jnp.float32)

    def rotate(value):
        high = value.astype(jnp.bfloat16)
        low = (value - high.astype(jnp.float32)).astype(jnp.bfloat16)
        return mul(high, table[...]) + mul(low, table[...])

    for step in range(nodes):
        if step == 0:
            own_hidden().wait()
        else:
            hid_copy(step).wait_recv()
        for part in range(rows // BLOCK):
            span = slice(part * BLOCK, (part + 1) * BLOCK)
            hid_t[step, span, :] = hid[step, :, span].T

    @pl.loop(0, chunks)
    def _(j):
        @pl.when(j + WINDOW < chunks)
        def _():
            for step in range(1, nodes):
                cot_copy(j + WINDOW, step).start()

        own_cot(j).wait()
        for step in range(1, nodes):
            cot_copy(j, step).wait_recv()
        expand = spread(j)

        @pl.loop(0, chips)
        def _(z):
            span = pl.ds(pl.multiple_of(z * tile, tile), tile)
            total = None
            for step in range(nodes):
                term = mul(hid_t[step, span, :], cot[j, step]).astype(jnp.bfloat16).astype(jnp.float32)
                total = term if total is None else total + term
            level = rotate(total) * mul(inverse[span, :], expand)
            level = jnp.clip(level, -7.0, 7.0).astype(jnp.bfloat16)
            levels[j, 0, z] = level[:final]
            levels[j, 1, z] = level[final:]

        pair_copy(j).start()
        pair_copy(j).wait_recv()

        @pl.loop(0, chips)
        def _(z):
            both = levels[j, core, z].astype(jnp.float32) + partner_in[j, z].astype(jnp.float32)
            pair[j, z] = both.astype(jnp.bfloat16)

        for step in range(1, chips):
            z_copy(j, step).start()

    own_rows = pl.ds(pl.multiple_of(replica * final, final), final)

    @pl.loop(0, chunks)
    def _(j):
        total = pair[j, chip].astype(jnp.float32)
        for step in range(1, chips):
            z_copy(j, step).wait_recv()
            total = total + arrived[j, step - 1].astype(jnp.float32)
        total = total * mul(forward[own_rows, :], spread(j))
        out[:, pl.ds(pl.multiple_of(j * chunk, BLOCK), chunk)] = rotate(total)

    for step in range(1, nodes):
        hid_copy(step).wait_send()

    @pl.loop(0, chunks)
    def _(j):
        for step in range(1, nodes):
            cot_copy(j, step).wait_send()
        pair_copy(j).wait_send()
        for step in range(1, chips):
            z_copy(j, step).wait_send()


def on_device(nodes, replicas, hidden, cotangent, scales):
    tokens, slab = hidden.shape
    width = cotangent.shape[1]
    chunk = 2 * BLOCK
    chunks = width // chunk
    rows = slab // nodes
    final = rows // replicas
    chips = replicas // 2
    bf16 = jnp.bfloat16
    dma = pltpu.SemaphoreType.DMA
    return pl.pallas_call(
        functools.partial(kernel, nodes, replicas, chunk),
        out_shape=jax.ShapeDtypeStruct((final, width), jnp.float32),
        in_specs=[
            pl.BlockSpec(memory_space=pl.ANY),
            pl.BlockSpec(memory_space=pl.ANY),
            pl.BlockSpec(memory_space=pltpu.VMEM),
        ],
        out_specs=pl.BlockSpec(memory_space=pltpu.VMEM),
        scratch_shapes=[
            pltpu.VMEM((nodes, tokens, rows), bf16),
            pltpu.VMEM((nodes, rows, tokens), bf16),
            pltpu.VMEM((chunks, nodes, tokens, chunk), bf16),
            pltpu.VMEM((chunk, chunk), bf16),
            pltpu.VMEM((rows, 2 * BLOCK), bf16),
            pltpu.VMEM((rows, 2 * BLOCK), bf16),
            pltpu.VMEM((chunks, 2, chips, final, chunk), bf16),
            pltpu.VMEM((chunks, chips, final, chunk), bf16),
            pltpu.VMEM((chunks, chips, final, chunk), bf16),
            pltpu.VMEM((chunks, chips - 1, final, chunk), bf16),
            dma((1 + chunks,)),
            dma((nodes - 1,)),
            dma((nodes - 1,)),
            dma((chunks, nodes - 1)),
            dma((chunks, nodes - 1)),
            dma((chunks,)),
            dma((chunks,)),
            dma((chunks, chips - 1)),
            dma((chunks, chips - 1)),
        ],
        compiler_params=pltpu.CompilerParams(
            collective_id=0, has_side_effects=True, vmem_limit_bytes=52 * 1024 * 1024
        ),
        cost_estimate=pl.CostEstimate(
            flops=2 * tokens * slab * width, bytes_accessed=2 * tokens * (slab + width), transcendentals=0
        ),
    )(hidden, cotangent, scales)


def solution(mesh):
    in_specs = (P(("node", "replica"), None), P(("node", "replica"), None), P("node", None))
    out_specs = P(("node", "replica"), None)
    return jax.shard_map(
        functools.partial(on_device, mesh.shape["node"], mesh.shape["replica"]),
        mesh=mesh, in_specs=in_specs, out_specs=out_specs, check_vma=False,
    )
```

```python
import functools
import math

import jax
import jax.numpy as jnp
from jax import lax
from jax.experimental import pallas as pl
from jax.experimental.pallas import tpu as pltpu
from jax.sharding import PartitionSpec as P

MESH = pl.DeviceIdType.MESH
BLOCK = 128
WINDOW = 4
AHEAD = 2
RELAY_LAG = 2
FINISH_LAG = 4


def kernel(
    nodes, replicas, chunk,
    hidden, cotangent, scales, out,
    hid, hid_t, cot, table, inverse, forward, levels, partner_in, pair, arrived, relay_in, merged,
    local_sem, hid_send, hid_recv, cot_send, cot_recv, pair_send, pair_recv, z_send, z_recv,
    forward_send, forward_recv, relay_send, relay_recv, cross_send, cross_recv,
):
    chips = replicas // 2
    tokens, slab = hidden.shape
    width = cotangent.shape[1]
    chunks = width // chunk
    rows = slab // nodes
    final = rows // replicas
    tile = 2 * final
    scale_cols = scales.shape[1]
    node = lax.axis_index("node")
    replica = lax.axis_index("replica")
    chip = replica // 2
    core = lax.rem(replica, 2)
    partner = chip * 2 + (1 - core)

    square = nodes == 4
    line = chips == 4
    node_y, node_x = node // 2, lax.rem(node, 2)
    side = chip // 2
    mate = side * 2 + (1 - lax.rem(chip, 2))
    far = 2 * (1 - side)
    inner = lax.rem(chip, 2) == 1 - side
    edge = lax.rem(chip, 2) == side
    direct = (1, 2) if square else tuple(range(1, nodes))
    halves = ((far, 2), (2 * side, 2)) if line else ((0, chips),)

    def peer_node(step):
        if square:
            across_x = 1 - node_x if step % 2 else node_x
            across_y = 1 - node_y if step // 2 else node_y
            return across_y * 2 + across_x
        return lax.rem(node + step, nodes)

    def peer_replica(step):
        return lax.rem(chip + step, chips) * 2 + core

    barrier = pltpu.get_barrier_semaphore()
    for step in range(1, nodes):
        pl.semaphore_signal(barrier, inc=1, device_id={"node": peer_node(step)}, device_id_type=MESH)
    pl.semaphore_signal(barrier, inc=1, device_id={"replica": partner}, device_id_type=MESH)
    for step in range(1, chips):
        pl.semaphore_signal(barrier, inc=1, device_id={"replica": peer_replica(step)}, device_id_type=MESH)

    def own_hidden():
        begin = pl.multiple_of(node * rows, BLOCK)
        return pltpu.make_async_copy(hidden.at[:, pl.ds(begin, rows)], hid.at[0], local_sem.at[0])

    def own_cot(j):
        begin = pl.multiple_of(j * chunk, BLOCK)
        return pltpu.make_async_copy(cotangent.at[:, pl.ds(begin, chunk)], cot.at[j, 0], local_sem.at[1 + j])

    def hid_copy(step):
        to = peer_node(step)
        begin = pl.multiple_of(to * rows, BLOCK)
        return pltpu.make_async_remote_copy(
            hidden.at[:, pl.ds(begin, rows)], hid.at[step], hid_send.at[step - 1], hid_recv.at[step - 1],
            device_id={"node": to}, device_id_type=MESH,
        )

    def cot_copy(j, step):
        begin = pl.multiple_of(j * chunk, BLOCK)
        return pltpu.make_async_remote_copy(
            cotangent.at[:, pl.ds(begin, chunk)], cot.at[j, step],
            cot_send.at[j, step - 1], cot_recv.at[j, step - 1],
            device_id={"node": peer_node(step)}, device_id_type=MESH,
        )

    def forward_copy(j, way):
        span = slice(way * (tokens // 2), (way + 1) * (tokens // 2))
        return pltpu.make_async_remote_copy(
            cot.at[j, 1 + way, span], cot.at[j, 3, span], forward_send.at[j, way], forward_recv.at[j, way],
            device_id={"node": peer_node(2 - way)}, device_id_type=MESH,
        )

    def pass_on(j):
        for way in range(2):
            cot_copy(j, 1 + way).wait_recv()
            forward_copy(j, way).start()

    def pair_copy(j, half):
        first, count = halves[half]
        return pltpu.make_async_remote_copy(
            levels.at[j, 1 - core, pl.ds(first, count)], partner_in.at[j, pl.ds(first, count)],
            pair_send.at[j, half], pair_recv.at[j, half],
            device_id={"replica": partner}, device_id_type=MESH,
        )

    def mate_copy(j):
        return pltpu.make_async_remote_copy(
            pair.at[j, mate], arrived.at[j, 0], z_send.at[j, 0], z_recv.at[j, 0],
            device_id={"replica": mate * 2 + core}, device_id_type=MESH,
        )

    def relay_copy(j):
        return pltpu.make_async_remote_copy(
            pair.at[j, pl.ds(far, 2)], relay_in.at[j], relay_send.at[j], relay_recv.at[j],
            device_id={"replica": mate * 2 + core}, device_id_type=MESH,
        )

    def cross_copy(j, k):
        return pltpu.make_async_remote_copy(
            merged.at[j, k], arrived.at[j, 1], cross_send.at[j, k], cross_recv.at[j],
            device_id={"replica": (far + k) * 2 + core}, device_id_type=MESH,
        )

    def relay(j):
        @pl.when(inner)
        def _():
            relay_copy(j).wait_recv()
            for k in range(2):
                both = pair[j, far + k].astype(jnp.float32) + relay_in[j, k].astype(jnp.float32)
                merged[j, k] = both.astype(jnp.bfloat16)
                cross_copy(j, k).start()

    def z_copy(j, step):
        to = lax.rem(chip + step, chips)
        return pltpu.make_async_remote_copy(
            pair.at[j, to], arrived.at[j, step - 1], z_send.at[j, step - 1], z_recv.at[j, step - 1],
            device_id={"replica": to * 2 + core}, device_id_type=MESH,
        )

    own_hidden().start()

    @pl.loop(0, chunks)
    def _(j):
        own_cot(j).start()

    pl.semaphore_wait(barrier, nodes - 1 + chips)
    for step in range(1, nodes):
        hid_copy(step).start()

    def send_cot(j):
        for step in direct:
            cot_copy(j, step).start()

    for j in range(AHEAD):
        send_cot(j)

    row_index = lax.broadcasted_iota(jnp.int32, (chunk, chunk), 0)
    col_index = lax.broadcasted_iota(jnp.int32, (chunk, chunk), 1)
    bits = jnp.bitwise_and(jnp.bitwise_and(row_index, col_index), BLOCK - 1)
    for shift in (4, 2, 1):
        bits = jnp.bitwise_xor(bits, jnp.right_shift(bits, shift))
    signs = 1.0 - 2.0 * jnp.bitwise_and(bits, 1).astype(jnp.float32)
    same = jnp.right_shift(row_index, 7) == jnp.right_shift(col_index, 7)
    table[...] = jnp.where(same, signs, 0.0).astype(jnp.bfloat16)

    def split_store(ref, value):
        high = value.astype(jnp.bfloat16)
        low = (value - high.astype(jnp.float32)).astype(jnp.bfloat16)
        ref[...] = jnp.zeros_like(ref)
        ref[:, :scale_cols] = high
        ref[:, BLOCK:BLOCK + scale_cols] = low

    norm = 1.0 / math.sqrt(BLOCK)
    split_store(inverse, norm / scales[...])
    split_store(forward, norm * scales[...])

    def spread(j):
        source = lax.broadcasted_iota(jnp.int32, (2 * BLOCK, chunk), 0)
        target = lax.broadcasted_iota(jnp.int32, (2 * BLOCK, chunk), 1)
        hit = jnp.bitwise_and(source, BLOCK - 1) == jnp.right_shift(target, 7) + j * (chunk // BLOCK)
        return jnp.where(hit, 1.0, 0.0).astype(jnp.bfloat16)

    def mul(left, right):
        return jnp.dot(left, right, preferred_element_type=jnp.float32)

    def rotate(value):
        high = value.astype(jnp.bfloat16)
        low = (value - high.astype(jnp.float32)).astype(jnp.bfloat16)
        return mul(high, table[...]) + mul(low, table[...])

    for step in range(nodes):
        if step == 0:
            own_hidden().wait()
        else:
            hid_copy(step).wait_recv()
        if step == 1:
            for j in range(AHEAD, WINDOW):
                send_cot(j)
        for part in range(rows // BLOCK):
            span = slice(part * BLOCK, (part + 1) * BLOCK)
            hid_t[step, span, :] = hid[step, :, span].T
        if square and step >= nodes - AHEAD:
            pass_on(step - (nodes - AHEAD))

    own_rows = pl.ds(pl.multiple_of(replica * final, final), final)

    def finish(j):
        total = pair[j, chip].astype(jnp.float32)
        if line:
            mate_copy(j).wait_recv()
            cross_copy(j, 0).wait_recv()
        for slot in range(arrived.shape[1]):
            if not line:
                z_copy(j, slot + 1).wait_recv()
            total = total + arrived[j, slot].astype(jnp.float32)
        total = total * mul(forward[own_rows, :], spread(j))
        out[:, pl.ds(pl.multiple_of(j * chunk, BLOCK), chunk)] = rotate(total)

    @pl.loop(0, chunks)
    def _(j):
        @pl.when(j + WINDOW < chunks)
        def _():
            send_cot(j + WINDOW)

        own_cot(j).wait()
        if square:
            @pl.when(j + AHEAD < chunks)
            def _():
                pass_on(j + AHEAD)

            for way in range(2):
                forward_copy(j, way).wait_recv()
        else:
            for step in direct:
                cot_copy(j, step).wait_recv()
        expand = spread(j)

        for half, (first, count) in enumerate(halves):
            @pl.loop(first, first + count)
            def _(z):
                span = pl.ds(pl.multiple_of(z * tile, tile), tile)
                total = None
                for step in range(nodes):
                    term = mul(hid_t[step, span, :], cot[j, step]).astype(jnp.bfloat16).astype(jnp.float32)
                    total = term if total is None else total + term
                level = rotate(total) * mul(inverse[span, :], expand)
                level = jnp.clip(level, -7.0, 7.0).astype(jnp.bfloat16)
                levels[j, 0, z] = level[:final]
                levels[j, 1, z] = level[final:]

            pair_copy(j, half).start()

        for half, (first, count) in enumerate(halves):
            pair_copy(j, half).wait_recv()

            @pl.loop(first, first + count)
            def _(z):
                both = levels[j, core, z].astype(jnp.float32) + partner_in[j, z].astype(jnp.float32)
                pair[j, z] = both.astype(jnp.bfloat16)

            if line and half == 0:
                @pl.when(edge)
                def _():
                    relay_copy(j).start()

        if line:
            mate_copy(j).start()

            @pl.when(j >= RELAY_LAG)
            def _():
                relay(j - RELAY_LAG)
        else:
            for step in range(1, chips):
                z_copy(j, step).start()

        @pl.when(j >= FINISH_LAG)
        def _():
            finish(j - FINISH_LAG)

    if line:
        @pl.loop(chunks - RELAY_LAG, chunks)
        def _(j):
            relay(j)

    @pl.loop(chunks - FINISH_LAG, chunks)
    def _(j):
        finish(j)

    for step in range(1, nodes):
        hid_copy(step).wait_send()

    @pl.loop(0, chunks)
    def _(j):
        for step in direct:
            cot_copy(j, step).wait_send()
        if square:
            for way in range(2):
                forward_copy(j, way).wait_send()
        for half in range(len(halves)):
            pair_copy(j, half).wait_send()
        if line:
            mate_copy(j).wait_send()

            @pl.when(edge)
            def _():
                relay_copy(j).wait_send()

            @pl.when(inner)
            def _():
                for k in range(2):
                    cross_copy(j, k).wait_send()
        else:
            for step in range(1, chips):
                z_copy(j, step).wait_send()


def on_device(nodes, replicas, hidden, cotangent, scales):
    tokens, slab = hidden.shape
    width = cotangent.shape[1]
    chunk = 2 * BLOCK
    chunks = width // chunk
    rows = slab // nodes
    final = rows // replicas
    chips = replicas // 2
    slots = 2 if chips == 4 else chips - 1
    bf16 = jnp.bfloat16
    dma = pltpu.SemaphoreType.DMA
    return pl.pallas_call(
        functools.partial(kernel, nodes, replicas, chunk),
        out_shape=jax.ShapeDtypeStruct((final, width), jnp.float32),
        in_specs=[
            pl.BlockSpec(memory_space=pl.ANY),
            pl.BlockSpec(memory_space=pl.ANY),
            pl.BlockSpec(memory_space=pltpu.VMEM),
        ],
        out_specs=pl.BlockSpec(memory_space=pltpu.VMEM),
        scratch_shapes=[
            pltpu.VMEM((nodes, tokens, rows), bf16),
            pltpu.VMEM((nodes, rows, tokens), bf16),
            pltpu.VMEM((chunks, nodes, tokens, chunk), bf16),
            pltpu.VMEM((chunk, chunk), bf16),
            pltpu.VMEM((rows, 2 * BLOCK), bf16),
            pltpu.VMEM((rows, 2 * BLOCK), bf16),
            pltpu.VMEM((chunks, 2, chips, final, chunk), bf16),
            pltpu.VMEM((chunks, chips, final, chunk), bf16),
            pltpu.VMEM((chunks, chips, final, chunk), bf16),
            pltpu.VMEM((chunks, slots, final, chunk), bf16),
            pltpu.VMEM((chunks, 2, final, chunk), bf16),
            pltpu.VMEM((chunks, 2, final, chunk), bf16),
            dma((1 + chunks,)),
            dma((nodes - 1,)),
            dma((nodes - 1,)),
            dma((chunks, nodes - 1)),
            dma((chunks, nodes - 1)),
            dma((chunks, 2)),
            dma((chunks, 2)),
            dma((chunks, slots)),
            dma((chunks, slots)),
            dma((chunks, 2)),
            dma((chunks, 2)),
            dma((chunks,)),
            dma((chunks,)),
            dma((chunks, 2)),
            dma((chunks,)),
        ],
        compiler_params=pltpu.CompilerParams(
            collective_id=0, has_side_effects=True, vmem_limit_bytes=52 * 1024 * 1024
        ),
        cost_estimate=pl.CostEstimate(
            flops=2 * tokens * slab * width, bytes_accessed=2 * tokens * (slab + width), transcendentals=0
        ),
    )(hidden, cotangent, scales)


def solution(mesh):
    in_specs = (P(("node", "replica"), None), P(("node", "replica"), None), P("node", None))
    out_specs = P(("node", "replica"), None)
    return jax.shard_map(
        functools.partial(on_device, mesh.shape["node"], mesh.shape["replica"]),
        mesh=mesh, in_specs=in_specs, out_specs=out_specs, check_vma=False,
    )
```

```python
import functools
import math

import jax
import jax.numpy as jnp
from jax import lax
from jax.experimental import pallas as pl
from jax.experimental.pallas import tpu as pltpu
from jax.sharding import PartitionSpec as P

MESH = pl.DeviceIdType.MESH
BLOCK = 128
WINDOW = 4
AHEAD = 2
RELAY_LAG = 2
FINISH_LAG = 4


def kernel(
    nodes, replicas, chunk,
    hidden, cotangent, scales, out,
    raw, hid, hid_t, cot, table, stage, inverse, forward, spread_inverse, levels, partner_in, pair, arrived, relay_in, merged,
    local_sem, hid_send, hid_recv, cot_send, cot_recv, pair_send, pair_recv, z_send, z_recv,
    forward_send, forward_recv, relay_send, relay_recv, cross_send, cross_recv,
):
    chips = replicas // 2
    tokens, slab = hidden.shape
    width = cotangent.shape[1]
    chunks = width // chunk
    rows = slab // nodes
    final = rows // replicas
    tile = 2 * final
    scale_cols = scales.shape[0]
    node = lax.axis_index("node")
    replica = lax.axis_index("replica")
    chip = replica // 2
    core = lax.rem(replica, 2)
    partner = chip * 2 + (1 - core)

    square = nodes == 4
    line = chips == 4
    node_y, node_x = node // 2, lax.rem(node, 2)
    side = chip // 2
    mate = side * 2 + (1 - lax.rem(chip, 2))
    far = 2 * (1 - side)
    inner = lax.rem(chip, 2) == 1 - side
    edge = lax.rem(chip, 2) == side
    direct = (1, 2) if square else tuple(range(1, nodes))
    halves = ((far, 2), (2 * side, 2)) if line else ((0, chips),)

    def peer_node(step):
        if square:
            across_x = 1 - node_x if step % 2 else node_x
            across_y = 1 - node_y if step // 2 else node_y
            return across_y * 2 + across_x
        return lax.rem(node + step, nodes)

    def peer_replica(step):
        return lax.rem(chip + step, chips) * 2 + core

    barrier = pltpu.get_barrier_semaphore()
    for step in range(1, nodes):
        pl.semaphore_signal(barrier, inc=1, device_id={"node": peer_node(step)}, device_id_type=MESH)
    pl.semaphore_signal(barrier, inc=1, device_id={"replica": partner}, device_id_type=MESH)
    for step in range(1, chips):
        pl.semaphore_signal(barrier, inc=1, device_id={"replica": peer_replica(step)}, device_id_type=MESH)

    def own_hidden():
        begin = pl.multiple_of(node * rows, BLOCK)
        return pltpu.make_async_copy(hidden.at[:, pl.ds(begin, rows)], hid.at[0], local_sem.at[0])

    def own_cot():
        return pltpu.make_async_copy(cotangent, raw, local_sem.at[1])

    def slot(step):
        return slice(step * tokens, (step + 1) * tokens)

    def hid_copy(step):
        to = peer_node(step)
        begin = pl.multiple_of(to * rows, BLOCK)
        return pltpu.make_async_remote_copy(
            hidden.at[:, pl.ds(begin, rows)], hid.at[step], hid_send.at[step - 1], hid_recv.at[step - 1],
            device_id={"node": to}, device_id_type=MESH,
        )

    def cot_copy(j, step):
        return pltpu.make_async_remote_copy(
            cot.at[j, slot(0)], cot.at[j, slot(step)],
            cot_send.at[j, step - 1], cot_recv.at[j, step - 1],
            device_id={"node": peer_node(step)}, device_id_type=MESH,
        )

    def forward_copy(j, way):
        part = tokens // 2
        return pltpu.make_async_remote_copy(
            cot.at[j, pl.ds((1 + way) * tokens + way * part, part)],
            cot.at[j, pl.ds(3 * tokens + way * part, part)], forward_send.at[j, way], forward_recv.at[j, way],
            device_id={"node": peer_node(2 - way)}, device_id_type=MESH,
        )

    def pass_on(j):
        for way in range(2):
            cot_copy(j, 1 + way).wait_recv()
            forward_copy(j, way).start()

    def pair_copy(j, half):
        first, count = halves[half]
        return pltpu.make_async_remote_copy(
            levels.at[j, 1 - core, pl.ds(first, count)], partner_in.at[j, pl.ds(first, count)],
            pair_send.at[j, half], pair_recv.at[j, half],
            device_id={"replica": partner}, device_id_type=MESH,
        )

    def mate_copy(j):
        return pltpu.make_async_remote_copy(
            pair.at[j, mate], arrived.at[j, 0], z_send.at[j, 0], z_recv.at[j, 0],
            device_id={"replica": mate * 2 + core}, device_id_type=MESH,
        )

    def relay_copy(j):
        return pltpu.make_async_remote_copy(
            pair.at[j, pl.ds(far, 2)], relay_in.at[j], relay_send.at[j], relay_recv.at[j],
            device_id={"replica": mate * 2 + core}, device_id_type=MESH,
        )

    def cross_copy(j, k):
        return pltpu.make_async_remote_copy(
            merged.at[j, k], arrived.at[j, 1], cross_send.at[j, k], cross_recv.at[j],
            device_id={"replica": (far + k) * 2 + core}, device_id_type=MESH,
        )

    def relay(j):
        @pl.when(inner)
        def _():
            relay_copy(j).wait_recv()
            for k in range(2):
                both = pair[j, far + k].astype(jnp.float32) + relay_in[j, k].astype(jnp.float32)
                merged[j, k] = both.astype(jnp.bfloat16)
                cross_copy(j, k).start()

    def z_copy(j, step):
        to = lax.rem(chip + step, chips)
        return pltpu.make_async_remote_copy(
            pair.at[j, to], arrived.at[j, step - 1], z_send.at[j, step - 1], z_recv.at[j, step - 1],
            device_id={"replica": to * 2 + core}, device_id_type=MESH,
        )

    own_hidden().start()

    own_cot().start()

    pl.semaphore_wait(barrier, nodes - 1 + chips)
    for step in range(1, nodes):
        hid_copy(step).start()

    def send_cot(j):
        for step in direct:
            cot_copy(j, step).start()

    row_index = lax.broadcasted_iota(jnp.int32, (chunk, chunk), 0)
    col_index = lax.broadcasted_iota(jnp.int32, (chunk, chunk), 1)
    bits = jnp.bitwise_and(jnp.bitwise_and(row_index, col_index), BLOCK - 1)
    for shift in (4, 2, 1):
        bits = jnp.bitwise_xor(bits, jnp.right_shift(bits, shift))
    signs = 1.0 - 2.0 * jnp.bitwise_and(bits, 1).astype(jnp.float32)
    same = jnp.right_shift(row_index, 7) == jnp.right_shift(col_index, 7)
    table[...] = jnp.where(same, signs, 0.0).astype(jnp.bfloat16)

    def spread(j):
        source = lax.broadcasted_iota(jnp.int32, (2 * BLOCK, chunk), 0)
        target = lax.broadcasted_iota(jnp.int32, (2 * BLOCK, chunk), 1)
        hit = jnp.bitwise_and(source, BLOCK - 1) == jnp.right_shift(target, 7) + j * (chunk // BLOCK)
        return jnp.where(hit, 1.0, 0.0).astype(jnp.bfloat16)

    def mul(left, right):
        return jnp.dot(left, right, preferred_element_type=jnp.float32)

    def rotate(value):
        high = value.astype(jnp.bfloat16)
        low = (value - high.astype(jnp.float32)).astype(jnp.bfloat16)
        return mul(high, table[...]) + mul(low, table[...])

    own_cot().wait()

    @pl.loop(0, chunks)
    def _(j):
        block = raw[:, pl.ds(pl.multiple_of(j * chunk, BLOCK), chunk)]
        cot[j, slot(0)] = mul(block, table[...]).astype(jnp.bfloat16)

    for j in range(AHEAD):
        send_cot(j)

    def split_store(ref, value):
        stage[...] = jnp.zeros_like(stage)
        stage[:scale_cols, :] = value
        for part in range(rows // BLOCK):
            span = slice(part * BLOCK, (part + 1) * BLOCK)
            turned = stage[:, span].T
            high = turned.astype(jnp.bfloat16)
            ref[span, :BLOCK] = high
            ref[span, BLOCK:] = (turned - high.astype(jnp.float32)).astype(jnp.bfloat16)

    norm = 1.0 / math.sqrt(BLOCK)
    split_store(inverse, norm / scales[...])
    split_store(forward, norm * scales[...])

    @pl.loop(0, chunks)
    def _(j):
        spread_inverse[j] = mul(inverse[...], spread(j))

    for step in range(nodes):
        if step == 0:
            own_hidden().wait()
        else:
            hid_copy(step).wait_recv()
        if step == 1:
            for j in range(AHEAD, WINDOW):
                send_cot(j)
        for part in range(rows // BLOCK):
            span = slice(part * BLOCK, (part + 1) * BLOCK)
            hid_t[span, slot(step)] = hid[step, :, span].T
        if square and step >= nodes - AHEAD:
            pass_on(step - (nodes - AHEAD))

    own_rows = pl.ds(pl.multiple_of(replica * final, final), final)

    def finish(j):
        total = pair[j, chip].astype(jnp.float32)
        if line:
            mate_copy(j).wait_recv()
            cross_copy(j, 0).wait_recv()
        for slot in range(arrived.shape[1]):
            if not line:
                z_copy(j, slot + 1).wait_recv()
            total = total + arrived[j, slot].astype(jnp.float32)
        total = total * mul(forward[own_rows, :], spread(j))
        out[:, pl.ds(pl.multiple_of(j * chunk, BLOCK), chunk)] = rotate(total)

    @pl.loop(0, chunks)
    def _(j):
        @pl.when(j + WINDOW < chunks)
        def _():
            send_cot(j + WINDOW)

        if square:
            @pl.when(j + AHEAD < chunks)
            def _():
                pass_on(j + AHEAD)

            for way in range(2):
                forward_copy(j, way).wait_recv()
        else:
            for step in direct:
                cot_copy(j, step).wait_recv()

        for half, (first, count) in enumerate(halves):
            span = pl.ds(pl.multiple_of(first * tile, tile), count * tile)
            level = mul(hid_t[span, :], cot[j]) * spread_inverse[j, span]
            level = jnp.clip(level, -7.0, 7.0).astype(jnp.bfloat16)
            for z in range(count):
                levels[j, 0, first + z] = level[z * tile:z * tile + final]
                levels[j, 1, first + z] = level[z * tile + final:(z + 1) * tile]

            pair_copy(j, half).start()

        for half, (first, count) in enumerate(halves):
            pair_copy(j, half).wait_recv()

            @pl.loop(first, first + count)
            def _(z):
                both = levels[j, core, z].astype(jnp.float32) + partner_in[j, z].astype(jnp.float32)
                pair[j, z] = both.astype(jnp.bfloat16)

            if line and half == 0:
                @pl.when(edge)
                def _():
                    relay_copy(j).start()

        if line:
            mate_copy(j).start()

            @pl.when(j >= RELAY_LAG)
            def _():
                relay(j - RELAY_LAG)
        else:
            for step in range(1, chips):
                z_copy(j, step).start()

        @pl.when(j >= FINISH_LAG)
        def _():
            finish(j - FINISH_LAG)

    if line:
        @pl.loop(chunks - RELAY_LAG, chunks)
        def _(j):
            relay(j)

    @pl.loop(chunks - FINISH_LAG, chunks)
    def _(j):
        finish(j)

    for step in range(1, nodes):
        hid_copy(step).wait_send()

    @pl.loop(0, chunks)
    def _(j):
        for step in direct:
            cot_copy(j, step).wait_send()
        if square:
            for way in range(2):
                forward_copy(j, way).wait_send()
        for half in range(len(halves)):
            pair_copy(j, half).wait_send()
        if line:
            mate_copy(j).wait_send()

            @pl.when(edge)
            def _():
                relay_copy(j).wait_send()

            @pl.when(inner)
            def _():
                for k in range(2):
                    cross_copy(j, k).wait_send()
        else:
            for step in range(1, chips):
                z_copy(j, step).wait_send()


def on_device(nodes, replicas, hidden, cotangent, scales):
    tokens, slab = hidden.shape
    width = cotangent.shape[1]
    chunk = 2 * BLOCK
    chunks = width // chunk
    rows = slab // nodes
    final = rows // replicas
    chips = replicas // 2
    slots = 2 if chips == 4 else chips - 1
    bf16 = jnp.bfloat16
    dma = pltpu.SemaphoreType.DMA
    return pl.pallas_call(
        functools.partial(kernel, nodes, replicas, chunk),
        out_shape=jax.ShapeDtypeStruct((final, width), jnp.float32),
        in_specs=[
            pl.BlockSpec(memory_space=pl.ANY),
            pl.BlockSpec(memory_space=pl.ANY),
            pl.BlockSpec(memory_space=pltpu.VMEM),
        ],
        out_specs=pl.BlockSpec(memory_space=pltpu.VMEM),
        scratch_shapes=[
            pltpu.VMEM((tokens, width), bf16),
            pltpu.VMEM((nodes, tokens, rows), bf16),
            pltpu.VMEM((rows, nodes * tokens), bf16),
            pltpu.VMEM((chunks, nodes * tokens, chunk), bf16),
            pltpu.VMEM((chunk, chunk), bf16),
            pltpu.VMEM((BLOCK, rows), jnp.float32),
            pltpu.VMEM((rows, 2 * BLOCK), bf16),
            pltpu.VMEM((rows, 2 * BLOCK), bf16),
            pltpu.VMEM((chunks, rows, chunk), jnp.float32),
            pltpu.VMEM((chunks, 2, chips, final, chunk), bf16),
            pltpu.VMEM((chunks, chips, final, chunk), bf16),
            pltpu.VMEM((chunks, chips, final, chunk), bf16),
            pltpu.VMEM((chunks, slots, final, chunk), bf16),
            pltpu.VMEM((chunks, 2, final, chunk), bf16),
            pltpu.VMEM((chunks, 2, final, chunk), bf16),
            dma((2,)),
            dma((nodes - 1,)),
            dma((nodes - 1,)),
            dma((chunks, nodes - 1)),
            dma((chunks, nodes - 1)),
            dma((chunks, 2)),
            dma((chunks, 2)),
            dma((chunks, slots)),
            dma((chunks, slots)),
            dma((chunks, 2)),
            dma((chunks, 2)),
            dma((chunks,)),
            dma((chunks,)),
            dma((chunks, 2)),
            dma((chunks,)),
        ],
        compiler_params=pltpu.CompilerParams(
            collective_id=0, has_side_effects=True, vmem_limit_bytes=52 * 1024 * 1024
        ),
        cost_estimate=pl.CostEstimate(
            flops=2 * tokens * slab * width, bytes_accessed=2 * tokens * (slab + width), transcendentals=0
        ),
    )(hidden, cotangent, scales.T)


def solution(mesh):
    in_specs = (P(("node", "replica"), None), P(("node", "replica"), None), P("node", None))
    out_specs = P(("node", "replica"), None)
    return jax.shard_map(
        functools.partial(on_device, mesh.shape["node"], mesh.shape["replica"]),
        mesh=mesh, in_specs=in_specs, out_specs=out_specs, check_vma=False,
    )
```

```python
import functools
import math

import jax
import jax.numpy as jnp
from jax import lax
from jax.experimental import pallas as pl
from jax.experimental.pallas import tpu as pltpu
from jax.sharding import PartitionSpec as P

MESH = pl.DeviceIdType.MESH
BLOCK = 128
WINDOW = 8
AHEAD = 4
PAIR_LAG = 1
RELAY_LAG = 4
FINISH_LAG = 8


def kernel(
    nodes, replicas, chunk,
    hidden, cotangent, scales, out,
    raw, scale, hid, hid_t, cot, table, stage, inverse, forward, spread_inverse, levels, partner_in, pair, arrived, relay_in, merged,
    local_sem, hid_send, hid_recv, cot_send, cot_recv, pair_send, pair_recv, z_send, z_recv,
    forward_send, forward_recv, relay_send, relay_recv, cross_send, cross_recv,
):
    chips = replicas // 2
    tokens, slab = hidden.shape
    width = cotangent.shape[1]
    chunks = width // chunk
    rows = slab // nodes
    final = rows // replicas
    tile = 2 * final
    scale_cols = scales.shape[0]
    node = lax.axis_index("node")
    replica = lax.axis_index("replica")
    chip = replica // 2
    core = lax.rem(replica, 2)
    partner = chip * 2 + (1 - core)

    square = nodes == 4
    line = chips == 4
    node_y, node_x = node // 2, lax.rem(node, 2)
    side = chip // 2
    mate = side * 2 + (1 - lax.rem(chip, 2))
    far = 2 * (1 - side)
    inner = lax.rem(chip, 2) == 1 - side
    edge = lax.rem(chip, 2) == side
    direct = (1, 2) if square else tuple(range(1, nodes))
    halves = ((far, 2), (2 * side, 2)) if line else ((0, chips),)

    def peer_node(step):
        if square:
            across_x = 1 - node_x if step % 2 else node_x
            across_y = 1 - node_y if step // 2 else node_y
            return across_y * 2 + across_x
        return lax.rem(node + step, nodes)

    def peer_replica(step):
        return lax.rem(chip + step, chips) * 2 + core

    barrier = pltpu.get_barrier_semaphore()
    for step in range(1, nodes):
        pl.semaphore_signal(barrier, inc=1, device_id={"node": peer_node(step)}, device_id_type=MESH)
    pl.semaphore_signal(barrier, inc=1, device_id={"replica": partner}, device_id_type=MESH)
    for step in range(1, chips):
        pl.semaphore_signal(barrier, inc=1, device_id={"replica": peer_replica(step)}, device_id_type=MESH)

    def own_hidden():
        begin = pl.multiple_of(node * rows, BLOCK)
        return pltpu.make_async_copy(hidden.at[:, pl.ds(begin, rows)], hid.at[0], local_sem.at[0])

    def own_cot():
        return pltpu.make_async_copy(cotangent, raw, local_sem.at[1])

    def slot(step):
        return slice(step * tokens, (step + 1) * tokens)

    def hid_copy(step):
        to = peer_node(step)
        begin = pl.multiple_of(to * rows, BLOCK)
        return pltpu.make_async_remote_copy(
            hidden.at[:, pl.ds(begin, rows)], hid.at[step], hid_send.at[step - 1], hid_recv.at[step - 1],
            device_id={"node": to}, device_id_type=MESH,
        )

    def cot_copy(j, step):
        return pltpu.make_async_remote_copy(
            cot.at[j, slot(0)], cot.at[j, slot(step)],
            cot_send.at[j, step - 1], cot_recv.at[j, step - 1],
            device_id={"node": peer_node(step)}, device_id_type=MESH,
        )

    def forward_copy(j, way):
        part = tokens // 2
        return pltpu.make_async_remote_copy(
            cot.at[j, pl.ds((1 + way) * tokens + way * part, part)],
            cot.at[j, pl.ds(3 * tokens + way * part, part)], forward_send.at[j, way], forward_recv.at[j, way],
            device_id={"node": peer_node(2 - way)}, device_id_type=MESH,
        )

    def pass_on(j):
        for way in range(2):
            cot_copy(j, 1 + way).wait_recv()
            forward_copy(j, way).start()

    def pair_copy(j, half):
        first, count = halves[half]
        return pltpu.make_async_remote_copy(
            levels.at[j, 1 - core, pl.ds(first, count)], partner_in.at[j, pl.ds(first, count)],
            pair_send.at[j, half], pair_recv.at[j, half],
            device_id={"replica": partner}, device_id_type=MESH,
        )

    def mate_copy(j):
        return pltpu.make_async_remote_copy(
            pair.at[j, mate], arrived.at[j, 0], z_send.at[j, 0], z_recv.at[j, 0],
            device_id={"replica": mate * 2 + core}, device_id_type=MESH,
        )

    def relay_copy(j):
        return pltpu.make_async_remote_copy(
            pair.at[j, pl.ds(far, 2)], relay_in.at[j], relay_send.at[j], relay_recv.at[j],
            device_id={"replica": mate * 2 + core}, device_id_type=MESH,
        )

    def cross_copy(j, k):
        return pltpu.make_async_remote_copy(
            merged.at[j, k], arrived.at[j, 1], cross_send.at[j, k], cross_recv.at[j],
            device_id={"replica": (far + k) * 2 + core}, device_id_type=MESH,
        )

    def relay(j):
        @pl.when(inner)
        def _():
            relay_copy(j).wait_recv()
            for k in range(2):
                both = pair[j, far + k].astype(jnp.float32) + relay_in[j, k].astype(jnp.float32)
                merged[j, k] = both.astype(jnp.bfloat16)
                cross_copy(j, k).start()

    def z_copy(j, step):
        to = lax.rem(chip + step, chips)
        return pltpu.make_async_remote_copy(
            pair.at[j, to], arrived.at[j, step - 1], z_send.at[j, step - 1], z_recv.at[j, step - 1],
            device_id={"replica": to * 2 + core}, device_id_type=MESH,
        )

    own_hidden().start()

    own_cot().start()
    own_scales = pltpu.make_async_copy(scales, scale, local_sem.at[2])
    own_scales.start()

    pl.semaphore_wait(barrier, nodes - 1 + chips)
    for step in range(1, nodes):
        hid_copy(step).start()

    def send_cot(j):
        for step in direct:
            cot_copy(j, step).start()

    row_index = lax.broadcasted_iota(jnp.int32, (chunk, chunk), 0)
    col_index = lax.broadcasted_iota(jnp.int32, (chunk, chunk), 1)
    bits = jnp.bitwise_and(jnp.bitwise_and(row_index, col_index), BLOCK - 1)
    for shift in (4, 2, 1):
        bits = jnp.bitwise_xor(bits, jnp.right_shift(bits, shift))
    signs = 1.0 - 2.0 * jnp.bitwise_and(bits, 1).astype(jnp.float32)
    same = jnp.right_shift(row_index, 7) == jnp.right_shift(col_index, 7)
    table[...] = jnp.where(same, signs, 0.0).astype(jnp.bfloat16)

    def spread(j):
        source = lax.broadcasted_iota(jnp.int32, (2 * BLOCK, chunk), 0)
        target = lax.broadcasted_iota(jnp.int32, (2 * BLOCK, chunk), 1)
        hit = jnp.bitwise_and(source, BLOCK - 1) == jnp.right_shift(target, 7) + j * (chunk // BLOCK)
        return jnp.where(hit, 1.0, 0.0).astype(jnp.bfloat16)

    def mul(left, right):
        return jnp.dot(left, right, preferred_element_type=jnp.float32)

    def rotate(value):
        high = value.astype(jnp.bfloat16)
        low = (value - high.astype(jnp.float32)).astype(jnp.bfloat16)
        return mul(high, table[...]) + mul(low, table[...])

    own_cot().wait()

    @pl.loop(0, chunks)
    def _(j):
        block = raw[:, pl.ds(pl.multiple_of(j * chunk, BLOCK), chunk)]
        cot[j, slot(0)] = mul(block, table[...]).astype(jnp.bfloat16)

    for j in range(AHEAD):
        send_cot(j)

    def split_store(ref, value):
        stage[...] = jnp.zeros_like(stage)
        stage[:scale_cols, :] = value
        for part in range(rows // BLOCK):
            span = slice(part * BLOCK, (part + 1) * BLOCK)
            turned = stage[:, span].T
            high = turned.astype(jnp.bfloat16)
            ref[span, :BLOCK] = high
            ref[span, BLOCK:] = (turned - high.astype(jnp.float32)).astype(jnp.bfloat16)

    norm = 1.0 / math.sqrt(BLOCK)
    own_scales.wait()
    split_store(inverse, norm / scale[...])
    split_store(forward, norm * scale[...])

    @pl.loop(0, chunks)
    def _(j):
        spread_inverse[j] = mul(inverse[...], spread(j))

    for step in range(nodes):
        if step == 0:
            own_hidden().wait()
        else:
            hid_copy(step).wait_recv()
        if step == 1:
            for j in range(AHEAD, WINDOW):
                send_cot(j)
        for part in range(rows // BLOCK):
            span = slice(part * BLOCK, (part + 1) * BLOCK)
            hid_t[span, slot(step)] = hid[step, :, span].T
        if square and step >= 2:
            for k in range(AHEAD // 2):
                pass_on((step - 2) * (AHEAD // 2) + k)

    own_rows = pl.ds(pl.multiple_of(replica * final, final), final)

    def finish(j):
        total = pair[j, chip].astype(jnp.float32)
        if line:
            mate_copy(j).wait_recv()
            cross_copy(j, 0).wait_recv()
        for slot in range(arrived.shape[1]):
            if not line:
                z_copy(j, slot + 1).wait_recv()
            total = total + arrived[j, slot].astype(jnp.float32)
        total = total * mul(forward[own_rows, :], spread(j))
        out[:, pl.ds(pl.multiple_of(j * chunk, BLOCK), chunk)] = rotate(total)

    def combine(j):
        for half, (first, count) in enumerate(halves):
            pair_copy(j, half).wait_recv()

            @pl.loop(first, first + count)
            def _(z):
                both = levels[j, core, z].astype(jnp.float32) + partner_in[j, z].astype(jnp.float32)
                pair[j, z] = both.astype(jnp.bfloat16)

            if line and half == 0:
                @pl.when(edge)
                def _():
                    relay_copy(j).start()

        if line:
            mate_copy(j).start()
        else:
            for step in range(1, chips):
                z_copy(j, step).start()

    @pl.loop(0, chunks)
    def _(j):
        @pl.when(j + WINDOW < chunks)
        def _():
            send_cot(j + WINDOW)

        if square:
            @pl.when(j + AHEAD < chunks)
            def _():
                pass_on(j + AHEAD)

            for way in range(2):
                forward_copy(j, way).wait_recv()
        else:
            for step in direct:
                cot_copy(j, step).wait_recv()

        for half, (first, count) in enumerate(halves):
            span = pl.ds(pl.multiple_of(first * tile, tile), count * tile)
            level = mul(hid_t[span, :], cot[j]) * spread_inverse[j, span]
            level = jnp.clip(level, -7.0, 7.0).astype(jnp.bfloat16)
            for z in range(count):
                levels[j, 0, first + z] = level[z * tile:z * tile + final]
                levels[j, 1, first + z] = level[z * tile + final:(z + 1) * tile]

            pair_copy(j, half).start()

        @pl.when(j >= PAIR_LAG)
        def _():
            combine(j - PAIR_LAG)

        if line:
            @pl.when(j >= RELAY_LAG)
            def _():
                relay(j - RELAY_LAG)

        @pl.when(j >= FINISH_LAG)
        def _():
            finish(j - FINISH_LAG)

    for j in range(chunks - PAIR_LAG, chunks):
        combine(j)

    if line:
        @pl.loop(chunks - RELAY_LAG, chunks)
        def _(j):
            relay(j)

    @pl.loop(chunks - FINISH_LAG, chunks)
    def _(j):
        finish(j)

    for step in range(1, nodes):
        hid_copy(step).wait_send()

    @pl.loop(0, chunks)
    def _(j):
        for step in direct:
            cot_copy(j, step).wait_send()
        if square:
            for way in range(2):
                forward_copy(j, way).wait_send()
        for half in range(len(halves)):
            pair_copy(j, half).wait_send()
        if line:
            mate_copy(j).wait_send()

            @pl.when(edge)
            def _():
                relay_copy(j).wait_send()

            @pl.when(inner)
            def _():
                for k in range(2):
                    cross_copy(j, k).wait_send()
        else:
            for step in range(1, chips):
                z_copy(j, step).wait_send()


def on_device(nodes, replicas, hidden, cotangent, scales):
    tokens, slab = hidden.shape
    width = cotangent.shape[1]
    chunk = BLOCK
    chunks = width // chunk
    rows = slab // nodes
    final = rows // replicas
    chips = replicas // 2
    slots = 2 if chips == 4 else chips - 1
    bf16 = jnp.bfloat16
    dma = pltpu.SemaphoreType.DMA
    return pl.pallas_call(
        functools.partial(kernel, nodes, replicas, chunk),
        out_shape=jax.ShapeDtypeStruct((final, width), jnp.float32),
        in_specs=[
            pl.BlockSpec(memory_space=pl.ANY),
            pl.BlockSpec(memory_space=pl.ANY),
            pl.BlockSpec(memory_space=pl.ANY),
        ],
        out_specs=pl.BlockSpec(memory_space=pltpu.VMEM),
        scratch_shapes=[
            pltpu.VMEM((tokens, width), bf16),
            pltpu.VMEM((scales.shape[1], rows), jnp.float32),
            pltpu.VMEM((nodes, tokens, rows), bf16),
            pltpu.VMEM((rows, nodes * tokens), bf16),
            pltpu.VMEM((chunks, nodes * tokens, chunk), bf16),
            pltpu.VMEM((chunk, chunk), bf16),
            pltpu.VMEM((BLOCK, rows), jnp.float32),
            pltpu.VMEM((rows, 2 * BLOCK), bf16),
            pltpu.VMEM((rows, 2 * BLOCK), bf16),
            pltpu.VMEM((chunks, rows, chunk), jnp.float32),
            pltpu.VMEM((chunks, 2, chips, final, chunk), bf16),
            pltpu.VMEM((chunks, chips, final, chunk), bf16),
            pltpu.VMEM((chunks, chips, final, chunk), bf16),
            pltpu.VMEM((chunks, slots, final, chunk), bf16),
            pltpu.VMEM((chunks, 2, final, chunk), bf16),
            pltpu.VMEM((chunks, 2, final, chunk), bf16),
            dma((3,)),
            dma((nodes - 1,)),
            dma((nodes - 1,)),
            dma((chunks, nodes - 1)),
            dma((chunks, nodes - 1)),
            dma((chunks, 2)),
            dma((chunks, 2)),
            dma((chunks, slots)),
            dma((chunks, slots)),
            dma((chunks, 2)),
            dma((chunks, 2)),
            dma((chunks,)),
            dma((chunks,)),
            dma((chunks, 2)),
            dma((chunks,)),
        ],
        compiler_params=pltpu.CompilerParams(
            collective_id=0, has_side_effects=True, vmem_limit_bytes=52 * 1024 * 1024
        ),
        cost_estimate=pl.CostEstimate(
            flops=2 * tokens * slab * width, bytes_accessed=2 * tokens * (slab + width), transcendentals=0
        ),
    )(hidden, cotangent, scales.T)


def solution(mesh):
    in_specs = (P(("node", "replica"), None), P(("node", "replica"), None), P("node", None))
    out_specs = P(("node", "replica"), None)
    return jax.shard_map(
        functools.partial(on_device, mesh.shape["node"], mesh.shape["replica"]),
        mesh=mesh, in_specs=in_specs, out_specs=out_specs, check_vma=False,
    )
```

```python
import functools
import math

import jax
import jax.numpy as jnp
from jax import lax
from jax.experimental import pallas as pl
from jax.experimental.pallas import tpu as pltpu
from jax.sharding import PartitionSpec as P

MESH = pl.DeviceIdType.MESH
BLOCK = 128
WINDOW = 4
AHEAD = 2
PAIR_LAG = 0
RELAY_LAG = 2
FINISH_LAG = 4


def kernel(
    nodes, replicas, chunk,
    hidden, cotangent, scales, out,
    raw, scale, hid, hid_t, cot, table, stage, inverse, forward, spread_inverse, levels, partner_in, pair, arrived, relay_in, merged,
    local_sem, hid_send, hid_recv, cot_send, cot_recv, pair_send, pair_recv, z_send, z_recv,
    forward_send, forward_recv, relay_send, relay_recv, cross_send, cross_recv,
):
    chips = replicas // 2
    tokens, slab = hidden.shape
    width = cotangent.shape[1]
    chunks = width // chunk
    rows = slab // nodes
    final = rows // replicas
    tile = 2 * final
    scale_cols = scales.shape[0]
    node = lax.axis_index("node")
    replica = lax.axis_index("replica")
    chip = replica // 2
    core = lax.rem(replica, 2)
    partner = chip * 2 + (1 - core)

    square = nodes == 4
    line = chips == 4
    node_y, node_x = node // 2, lax.rem(node, 2)
    side = chip // 2
    mate = side * 2 + (1 - lax.rem(chip, 2))
    far = 2 * (1 - side)
    inner = lax.rem(chip, 2) == 1 - side
    edge = lax.rem(chip, 2) == side
    direct = (1, 2) if square else tuple(range(1, nodes))
    halves = ((far, 2), (2 * side, 2)) if line else ((0, chips),)

    def peer_node(step):
        if square:
            across_x = 1 - node_x if step % 2 else node_x
            across_y = 1 - node_y if step // 2 else node_y
            return across_y * 2 + across_x
        return lax.rem(node + step, nodes)

    def peer_replica(step):
        return lax.rem(chip + step, chips) * 2 + core

    barrier = pltpu.get_barrier_semaphore()
    for step in range(1, nodes):
        pl.semaphore_signal(barrier, inc=1, device_id={"node": peer_node(step)}, device_id_type=MESH)
    pl.semaphore_signal(barrier, inc=1, device_id={"replica": partner}, device_id_type=MESH)
    for step in range(1, chips):
        pl.semaphore_signal(barrier, inc=1, device_id={"replica": peer_replica(step)}, device_id_type=MESH)

    def own_hidden():
        begin = pl.multiple_of(node * rows, BLOCK)
        return pltpu.make_async_copy(hidden.at[:, pl.ds(begin, rows)], hid.at[0], local_sem.at[0])

    def own_cot():
        return pltpu.make_async_copy(cotangent, raw, local_sem.at[1])

    def slot(step):
        return slice(step * tokens, (step + 1) * tokens)

    def hid_copy(step):
        to = peer_node(step)
        begin = pl.multiple_of(to * rows, BLOCK)
        return pltpu.make_async_remote_copy(
            hidden.at[:, pl.ds(begin, rows)], hid.at[step], hid_send.at[step - 1], hid_recv.at[step - 1],
            device_id={"node": to}, device_id_type=MESH,
        )

    def cot_copy(j, step):
        return pltpu.make_async_remote_copy(
            cot.at[j, slot(0)], cot.at[j, slot(step)],
            cot_send.at[j, step - 1], cot_recv.at[j, step - 1],
            device_id={"node": peer_node(step)}, device_id_type=MESH,
        )

    def forward_copy(j, way):
        part = tokens // 2
        return pltpu.make_async_remote_copy(
            cot.at[j, pl.ds((1 + way) * tokens + way * part, part)],
            cot.at[j, pl.ds(3 * tokens + way * part, part)], forward_send.at[j, way], forward_recv.at[j, way],
            device_id={"node": peer_node(2 - way)}, device_id_type=MESH,
        )

    def pass_on(j):
        for way in range(2):
            cot_copy(j, 1 + way).wait_recv()
            forward_copy(j, way).start()

    def pair_copy(j, half):
        first, count = halves[half]
        return pltpu.make_async_remote_copy(
            levels.at[j, 1 - core, pl.ds(first, count)], partner_in.at[j, pl.ds(first, count)],
            pair_send.at[j, half], pair_recv.at[j, half],
            device_id={"replica": partner}, device_id_type=MESH,
        )

    def mate_copy(j):
        return pltpu.make_async_remote_copy(
            pair.at[j, mate], arrived.at[j, 0], z_send.at[j, 0], z_recv.at[j, 0],
            device_id={"replica": mate * 2 + core}, device_id_type=MESH,
        )

    def relay_copy(j):
        return pltpu.make_async_remote_copy(
            pair.at[j, pl.ds(far, 2)], relay_in.at[j], relay_send.at[j], relay_recv.at[j],
            device_id={"replica": mate * 2 + core}, device_id_type=MESH,
        )

    def cross_copy(j, k):
        return pltpu.make_async_remote_copy(
            merged.at[j, k], arrived.at[j, 1], cross_send.at[j, k], cross_recv.at[j],
            device_id={"replica": (far + k) * 2 + core}, device_id_type=MESH,
        )

    def relay(j):
        @pl.when(inner)
        def _():
            relay_copy(j).wait_recv()
            for k in range(2):
                both = pair[j, far + k].astype(jnp.float32) + relay_in[j, k].astype(jnp.float32)
                merged[j, k] = both.astype(jnp.bfloat16)
                cross_copy(j, k).start()

    def z_copy(j, step):
        to = lax.rem(chip + step, chips)
        return pltpu.make_async_remote_copy(
            pair.at[j, to], arrived.at[j, step - 1], z_send.at[j, step - 1], z_recv.at[j, step - 1],
            device_id={"replica": to * 2 + core}, device_id_type=MESH,
        )

    own_hidden().start()

    own_cot().start()
    own_scales = pltpu.make_async_copy(scales, scale, local_sem.at[2])
    own_scales.start()

    pl.semaphore_wait(barrier, nodes - 1 + chips)
    for step in reversed(range(1, nodes)):
        hid_copy(step).start()

    def send_cot(j):
        for step in direct:
            cot_copy(j, step).start()

    row_index = lax.broadcasted_iota(jnp.int32, (chunk, chunk), 0)
    col_index = lax.broadcasted_iota(jnp.int32, (chunk, chunk), 1)
    bits = jnp.bitwise_and(jnp.bitwise_and(row_index, col_index), BLOCK - 1)
    for shift in (4, 2, 1):
        bits = jnp.bitwise_xor(bits, jnp.right_shift(bits, shift))
    signs = 1.0 - 2.0 * jnp.bitwise_and(bits, 1).astype(jnp.float32)
    same = jnp.right_shift(row_index, 7) == jnp.right_shift(col_index, 7)
    table[...] = jnp.where(same, signs, 0.0).astype(jnp.bfloat16)

    def spread(j):
        source = lax.broadcasted_iota(jnp.int32, (2 * BLOCK, chunk), 0)
        target = lax.broadcasted_iota(jnp.int32, (2 * BLOCK, chunk), 1)
        hit = jnp.bitwise_and(source, BLOCK - 1) == jnp.right_shift(target, 7) + j * (chunk // BLOCK)
        return jnp.where(hit, 1.0, 0.0).astype(jnp.bfloat16)

    def mul(left, right):
        return jnp.dot(left, right, preferred_element_type=jnp.float32)

    def rotate(value):
        high = value.astype(jnp.bfloat16)
        low = (value - high.astype(jnp.float32)).astype(jnp.bfloat16)
        return mul(high, table[...]) + mul(low, table[...])

    own_cot().wait()

    @pl.loop(0, chunks)
    def _(j):
        block = raw[:, pl.ds(pl.multiple_of(j * chunk, BLOCK), chunk)]
        cot[j, slot(0)] = mul(block, table[...]).astype(jnp.bfloat16)

    def split_store(ref, value):
        stage[...] = jnp.zeros_like(stage)
        stage[:scale_cols, :] = value
        for part in range(rows // BLOCK):
            span = slice(part * BLOCK, (part + 1) * BLOCK)
            turned = stage[:, span].T
            high = turned.astype(jnp.bfloat16)
            ref[span, :BLOCK] = high
            ref[span, BLOCK:] = (turned - high.astype(jnp.float32)).astype(jnp.bfloat16)

    norm = 1.0 / math.sqrt(BLOCK)
    own_scales.wait()
    split_store(inverse, norm / scale[...])
    split_store(forward, norm * scale[...])

    @pl.loop(0, chunks)
    def _(j):
        spread_inverse[j] = mul(inverse[...], spread(j))

    def turn(step):
        for part in range(rows // BLOCK):
            span = slice(part * BLOCK, (part + 1) * BLOCK)
            hid_t[span, slot(step)] = hid[step, :, span].T

    own_hidden().wait()
    turn(0)
    for step in direct:
        hid_copy(step).wait_recv()
    for j in range(AHEAD):
        send_cot(j)
    for step in direct:
        turn(step)
    if square:
        hid_copy(3).wait_recv()
        for j in range(AHEAD):
            pass_on(j)
            send_cot(j + AHEAD)
        turn(3)
    else:
        for j in range(AHEAD, WINDOW):
            send_cot(j)

    own_rows = pl.ds(pl.multiple_of(replica * final, final), final)

    def finish(j):
        total = pair[j, chip].astype(jnp.float32)
        if line:
            mate_copy(j).wait_recv()
            cross_copy(j, 0).wait_recv()
        for slot in range(arrived.shape[1]):
            if not line:
                z_copy(j, slot + 1).wait_recv()
            total = total + arrived[j, slot].astype(jnp.float32)
        total = total * mul(forward[own_rows, :], spread(j))
        out[:, pl.ds(pl.multiple_of(j * chunk, BLOCK), chunk)] = rotate(total)

    def combine(j):
        for half, (first, count) in enumerate(halves):
            pair_copy(j, half).wait_recv()

            @pl.loop(first, first + count)
            def _(z):
                both = levels[j, core, z].astype(jnp.float32) + partner_in[j, z].astype(jnp.float32)
                pair[j, z] = both.astype(jnp.bfloat16)

            if line and half == 0:
                @pl.when(edge)
                def _():
                    relay_copy(j).start()

        if line:
            mate_copy(j).start()
        else:
            for step in range(1, chips):
                z_copy(j, step).start()

    @pl.loop(0, chunks)
    def _(j):
        if square:
            @pl.when(j + AHEAD < chunks)
            def _():
                pass_on(j + AHEAD)

        @pl.when(j + WINDOW < chunks)
        def _():
            send_cot(j + WINDOW)

        if square:
            for way in range(2):
                forward_copy(j, way).wait_recv()
        else:
            for step in direct:
                cot_copy(j, step).wait_recv()

        for half, (first, count) in enumerate(halves):
            span = pl.ds(pl.multiple_of(first * tile, tile), count * tile)
            level = mul(hid_t[span, :], cot[j]) * spread_inverse[j, span]
            level = jnp.clip(level, -7.0, 7.0).astype(jnp.bfloat16)
            for z in range(count):
                levels[j, 0, first + z] = level[z * tile:z * tile + final]
                levels[j, 1, first + z] = level[z * tile + final:(z + 1) * tile]

            pair_copy(j, half).start()

        @pl.when(j >= PAIR_LAG)
        def _():
            combine(j - PAIR_LAG)

        if line:
            @pl.when(j >= RELAY_LAG)
            def _():
                relay(j - RELAY_LAG)

        @pl.when(j >= FINISH_LAG)
        def _():
            finish(j - FINISH_LAG)

    for j in range(chunks - PAIR_LAG, chunks):
        combine(j)

    if line:
        @pl.loop(chunks - RELAY_LAG, chunks)
        def _(j):
            relay(j)

    @pl.loop(chunks - FINISH_LAG, chunks)
    def _(j):
        finish(j)

    for step in range(1, nodes):
        hid_copy(step).wait_send()

    @pl.loop(0, chunks)
    def _(j):
        for step in direct:
            cot_copy(j, step).wait_send()
        if square:
            for way in range(2):
                forward_copy(j, way).wait_send()
        for half in range(len(halves)):
            pair_copy(j, half).wait_send()
        if line:
            mate_copy(j).wait_send()

            @pl.when(edge)
            def _():
                relay_copy(j).wait_send()

            @pl.when(inner)
            def _():
                for k in range(2):
                    cross_copy(j, k).wait_send()
        else:
            for step in range(1, chips):
                z_copy(j, step).wait_send()


def on_device(nodes, replicas, hidden, cotangent, scales):
    tokens, slab = hidden.shape
    width = cotangent.shape[1]
    chunk = 2 * BLOCK
    chunks = width // chunk
    rows = slab // nodes
    final = rows // replicas
    chips = replicas // 2
    slots = 2 if chips == 4 else chips - 1
    bf16 = jnp.bfloat16
    dma = pltpu.SemaphoreType.DMA
    return pl.pallas_call(
        functools.partial(kernel, nodes, replicas, chunk),
        out_shape=jax.ShapeDtypeStruct((final, width), jnp.float32),
        in_specs=[
            pl.BlockSpec(memory_space=pl.ANY),
            pl.BlockSpec(memory_space=pl.ANY),
            pl.BlockSpec(memory_space=pl.ANY),
        ],
        out_specs=pl.BlockSpec(memory_space=pltpu.VMEM),
        scratch_shapes=[
            pltpu.VMEM((tokens, width), bf16),
            pltpu.VMEM((scales.shape[1], rows), jnp.float32),
            pltpu.VMEM((nodes, tokens, rows), bf16),
            pltpu.VMEM((rows, nodes * tokens), bf16),
            pltpu.VMEM((chunks, nodes * tokens, chunk), bf16),
            pltpu.VMEM((chunk, chunk), bf16),
            pltpu.VMEM((BLOCK, rows), jnp.float32),
            pltpu.VMEM((rows, 2 * BLOCK), bf16),
            pltpu.VMEM((rows, 2 * BLOCK), bf16),
            pltpu.VMEM((chunks, rows, chunk), jnp.float32),
            pltpu.VMEM((chunks, 2, chips, final, chunk), bf16),
            pltpu.VMEM((chunks, chips, final, chunk), bf16),
            pltpu.VMEM((chunks, chips, final, chunk), bf16),
            pltpu.VMEM((chunks, slots, final, chunk), bf16),
            pltpu.VMEM((chunks, 2, final, chunk), bf16),
            pltpu.VMEM((chunks, 2, final, chunk), bf16),
            dma((3,)),
            dma((nodes - 1,)),
            dma((nodes - 1,)),
            dma((chunks, nodes - 1)),
            dma((chunks, nodes - 1)),
            dma((chunks, 2)),
            dma((chunks, 2)),
            dma((chunks, slots)),
            dma((chunks, slots)),
            dma((chunks, 2)),
            dma((chunks, 2)),
            dma((chunks,)),
            dma((chunks,)),
            dma((chunks, 2)),
            dma((chunks,)),
        ],
        compiler_params=pltpu.CompilerParams(
            collective_id=0, has_side_effects=True, vmem_limit_bytes=52 * 1024 * 1024
        ),
        cost_estimate=pl.CostEstimate(
            flops=2 * tokens * slab * width, bytes_accessed=2 * tokens * (slab + width), transcendentals=0
        ),
    )(hidden, cotangent, scales.T)


def solution(mesh):
    in_specs = (P(("node", "replica"), None), P(("node", "replica"), None), P("node", None))
    out_specs = P(("node", "replica"), None)
    return jax.shard_map(
        functools.partial(on_device, mesh.shape["node"], mesh.shape["replica"]),
        mesh=mesh, in_specs=in_specs, out_specs=out_specs, check_vma=False,
    )
```

```python
import functools
import math

import jax
import jax.numpy as jnp
from jax import lax
from jax.experimental import pallas as pl
from jax.experimental.pallas import tpu as pltpu
from jax.sharding import PartitionSpec as P

MESH = pl.DeviceIdType.MESH
BLOCK = 128
WINDOW = 4
AHEAD = 2
LATE_HIDDEN = 3
RELAY_LAG = 2
FINISH_LAG = 4


def kernel(
    nodes, replicas, chunk,
    hidden, cotangent, scales, out,
    raw, scale, hid, hid_t, cot, table, stage, inverse, forward, spread_inverse, levels, partner_in, pair, arrived, relay_in, merged,
    local_sem, hid_send, hid_recv, cot_send, cot_recv, pair_send, pair_recv, z_send, z_recv,
    forward_send, forward_recv, relay_send, relay_recv, cross_send, cross_recv,
):
    chips = replicas // 2
    tokens, slab = hidden.shape
    width = cotangent.shape[1]
    chunks = width // chunk
    rows = slab // nodes
    final = rows // replicas
    tile = 2 * final
    scale_cols = scales.shape[0]
    node = lax.axis_index("node")
    replica = lax.axis_index("replica")
    chip = replica // 2
    core = lax.rem(replica, 2)
    partner = chip * 2 + (1 - core)

    square = nodes == 4
    line = chips == 4
    node_y, node_x = node // 2, lax.rem(node, 2)
    side = chip // 2
    mate = side * 2 + (1 - lax.rem(chip, 2))
    far = 2 * (1 - side)
    inner = lax.rem(chip, 2) == 1 - side
    edge = lax.rem(chip, 2) == side
    direct = (1, 2) if square else tuple(range(1, nodes))
    parts = ((far, 2), (mate, 1), (chip, 1)) if line else ((0, chips),)
    early = parts[:2]

    def peer_node(step):
        if square:
            across_x = 1 - node_x if step % 2 else node_x
            across_y = 1 - node_y if step // 2 else node_y
            return across_y * 2 + across_x
        return lax.rem(node + step, nodes)

    def peer_replica(step):
        return lax.rem(chip + step, chips) * 2 + core

    barrier = pltpu.get_barrier_semaphore()
    for step in range(1, nodes):
        pl.semaphore_signal(barrier, inc=1, device_id={"node": peer_node(step)}, device_id_type=MESH)
    pl.semaphore_signal(barrier, inc=1, device_id={"replica": partner}, device_id_type=MESH)
    for step in range(1, chips):
        pl.semaphore_signal(barrier, inc=1, device_id={"replica": peer_replica(step)}, device_id_type=MESH)

    def own_hidden():
        begin = pl.multiple_of(node * rows, BLOCK)
        return pltpu.make_async_copy(hidden.at[:, pl.ds(begin, rows)], hid.at[0], local_sem.at[0])

    def own_cot():
        return pltpu.make_async_copy(cotangent, raw, local_sem.at[1])

    def slot(step):
        return slice(step * tokens, (step + 1) * tokens)

    def hid_copy(step, part):
        to = peer_node(step)
        first, count = parts[part]
        source = pl.multiple_of(to * rows + first * tile, BLOCK)
        target = pl.multiple_of(first * tile, BLOCK)
        return pltpu.make_async_remote_copy(
            hidden.at[:, pl.ds(source, count * tile)], hid.at[step, :, pl.ds(target, count * tile)],
            hid_send.at[step - 1, part], hid_recv.at[step - 1, part],
            device_id={"node": to}, device_id_type=MESH,
        )

    def send_hid(part):
        for step in reversed(range(1, nodes)):
            hid_copy(step, part).start()

    def cot_copy(j, step):
        return pltpu.make_async_remote_copy(
            cot.at[j, slot(0)], cot.at[j, slot(step)],
            cot_send.at[j, step - 1], cot_recv.at[j, step - 1],
            device_id={"node": peer_node(step)}, device_id_type=MESH,
        )

    def forward_copy(j, way):
        part = tokens // 2
        return pltpu.make_async_remote_copy(
            cot.at[j, pl.ds((1 + way) * tokens + way * part, part)],
            cot.at[j, pl.ds(3 * tokens + way * part, part)], forward_send.at[j, way], forward_recv.at[j, way],
            device_id={"node": peer_node(2 - way)}, device_id_type=MESH,
        )

    def pass_on(j):
        for way in range(2):
            cot_copy(j, 1 + way).wait_recv()
            forward_copy(j, way).start()

    def pair_copy(j, half):
        first, count = parts[half]
        return pltpu.make_async_remote_copy(
            levels.at[j, 1 - core, pl.ds(first, count)], partner_in.at[j, pl.ds(first, count)],
            pair_send.at[j, half], pair_recv.at[j, half],
            device_id={"replica": partner}, device_id_type=MESH,
        )

    def mate_copy(j):
        return pltpu.make_async_remote_copy(
            pair.at[j, mate], arrived.at[j, 0], z_send.at[j, 0], z_recv.at[j, 0],
            device_id={"replica": mate * 2 + core}, device_id_type=MESH,
        )

    def relay_copy(j):
        return pltpu.make_async_remote_copy(
            pair.at[j, pl.ds(far, 2)], relay_in.at[j], relay_send.at[j], relay_recv.at[j],
            device_id={"replica": mate * 2 + core}, device_id_type=MESH,
        )

    def cross_copy(j, k):
        return pltpu.make_async_remote_copy(
            merged.at[j, k], arrived.at[j, 1], cross_send.at[j, k], cross_recv.at[j],
            device_id={"replica": (far + k) * 2 + core}, device_id_type=MESH,
        )

    def relay(j):
        @pl.when(inner)
        def _():
            relay_copy(j).wait_recv()
            for k in range(2):
                both = pair[j, far + k].astype(jnp.float32) + relay_in[j, k].astype(jnp.float32)
                merged[j, k] = both.astype(jnp.bfloat16)
                cross_copy(j, k).start()

    def z_copy(j, step):
        to = lax.rem(chip + step, chips)
        return pltpu.make_async_remote_copy(
            pair.at[j, to], arrived.at[j, step - 1], z_send.at[j, step - 1], z_recv.at[j, step - 1],
            device_id={"replica": to * 2 + core}, device_id_type=MESH,
        )

    own_hidden().start()

    own_cot().start()
    own_scales = pltpu.make_async_copy(scales, scale, local_sem.at[2])
    own_scales.start()

    pl.semaphore_wait(barrier, nodes - 1 + chips)
    for part in range(len(early)):
        send_hid(part)

    def send_cot(j):
        for step in direct:
            cot_copy(j, step).start()

    row_index = lax.broadcasted_iota(jnp.int32, (chunk, chunk), 0)
    col_index = lax.broadcasted_iota(jnp.int32, (chunk, chunk), 1)
    bits = jnp.bitwise_and(jnp.bitwise_and(row_index, col_index), BLOCK - 1)
    for shift in (4, 2, 1):
        bits = jnp.bitwise_xor(bits, jnp.right_shift(bits, shift))
    signs = 1.0 - 2.0 * jnp.bitwise_and(bits, 1).astype(jnp.float32)
    same = jnp.right_shift(row_index, 7) == jnp.right_shift(col_index, 7)
    table[...] = jnp.where(same, signs, 0.0).astype(jnp.bfloat16)

    def spread(j):
        source = lax.broadcasted_iota(jnp.int32, (2 * BLOCK, chunk), 0)
        target = lax.broadcasted_iota(jnp.int32, (2 * BLOCK, chunk), 1)
        hit = jnp.bitwise_and(source, BLOCK - 1) == jnp.right_shift(target, 7) + j * (chunk // BLOCK)
        return jnp.where(hit, 1.0, 0.0).astype(jnp.bfloat16)

    def mul(left, right):
        return jnp.dot(left, right, preferred_element_type=jnp.float32)

    def rotate(value):
        high = value.astype(jnp.bfloat16)
        low = (value - high.astype(jnp.float32)).astype(jnp.bfloat16)
        return mul(high, table[...]) + mul(low, table[...])

    own_cot().wait()

    @pl.loop(0, chunks)
    def _(j):
        block = raw[:, pl.ds(pl.multiple_of(j * chunk, BLOCK), chunk)]
        cot[j, slot(0)] = mul(block, table[...]).astype(jnp.bfloat16)

    def split_store(ref, value):
        stage[...] = jnp.zeros_like(stage)
        stage[:scale_cols, :] = value
        for part in range(rows // BLOCK):
            span = slice(part * BLOCK, (part + 1) * BLOCK)
            turned = stage[:, span].T
            high = turned.astype(jnp.bfloat16)
            ref[span, :BLOCK] = high
            ref[span, BLOCK:] = (turned - high.astype(jnp.float32)).astype(jnp.bfloat16)

    norm = 1.0 / math.sqrt(BLOCK)
    own_scales.wait()
    split_store(inverse, norm / scale[...])
    split_store(forward, norm * scale[...])

    @pl.loop(0, chunks)
    def _(j):
        spread_inverse[j] = mul(inverse[...], spread(j))

    def turn(step, part):
        first, count = parts[part]
        for piece in range(count * tile // BLOCK):
            span = pl.ds(pl.multiple_of(first * tile + piece * BLOCK, BLOCK), BLOCK)
            hid_t[span, slot(step)] = hid[step, :, span].T

    own_hidden().wait()
    for part in range(len(parts)):
        turn(0, part)
    for part in range(len(early)):
        for step in direct:
            hid_copy(step, part).wait_recv()
    for j in range(AHEAD):
        send_cot(j)
    for part in range(len(early)):
        for step in direct:
            turn(step, part)
    if square:
        for part in range(len(early)):
            hid_copy(3, part).wait_recv()
        for j in range(AHEAD):
            pass_on(j)
            send_cot(j + AHEAD)
        for part in range(len(early)):
            turn(3, part)
    else:
        for j in range(AHEAD, WINDOW):
            send_cot(j)

    own_rows = pl.ds(pl.multiple_of(replica * final, final), final)

    def finish(j):
        if line:
            pair_copy(j, 2).wait_recv()
            mate_copy(j).wait_recv()
            cross_copy(j, 0).wait_recv()
            total = levels[j, core, chip].astype(jnp.float32) + partner_in[j, chip].astype(jnp.float32)
        else:
            total = pair[j, chip].astype(jnp.float32)
        for k in range(arrived.shape[1]):
            if not line:
                z_copy(j, k + 1).wait_recv()
            total = total + arrived[j, k].astype(jnp.float32)
        total = total * mul(forward[own_rows, :], spread(j))
        out[:, pl.ds(pl.multiple_of(j * chunk, BLOCK), chunk)] = rotate(total)

    def product(j, part):
        first, count = parts[part]
        span = pl.ds(pl.multiple_of(first * tile, tile), count * tile)
        level = mul(hid_t[span, :], cot[j]) * spread_inverse[j, span]
        level = jnp.clip(level, -7.0, 7.0).astype(jnp.bfloat16)
        for z in range(count):
            levels[j, 0, first + z] = level[z * tile:z * tile + final]
            levels[j, 1, first + z] = level[z * tile + final:(z + 1) * tile]
        pair_copy(j, part).start()

    def combine(j):
        for part, (first, count) in enumerate(early):
            pair_copy(j, part).wait_recv()
            for z in range(count):
                both = levels[j, core, first + z].astype(jnp.float32) + partner_in[j, first + z].astype(jnp.float32)
                pair[j, first + z] = both.astype(jnp.bfloat16)

            if line and part == 0:
                @pl.when(edge)
                def _():
                    relay_copy(j).start()

        if line:
            mate_copy(j).start()
        else:
            for step in range(1, chips):
                z_copy(j, step).start()

    @pl.loop(0, chunks)
    def _(j):
        if square:
            @pl.when(j + AHEAD < chunks)
            def _():
                pass_on(j + AHEAD)

        @pl.when(j + WINDOW < chunks)
        def _():
            send_cot(j + WINDOW)

        if square:
            for way in range(2):
                forward_copy(j, way).wait_recv()
        else:
            for step in direct:
                cot_copy(j, step).wait_recv()

        if line:
            @pl.when(j == chunks - LATE_HIDDEN)
            def _():
                send_hid(2)

        for part in range(len(early)):
            product(j, part)
        combine(j)

        if line:
            @pl.when(j >= RELAY_LAG)
            def _():
                relay(j - RELAY_LAG)
        else:
            @pl.when(j >= FINISH_LAG)
            def _():
                finish(j - FINISH_LAG)

    if line:
        @pl.loop(chunks - RELAY_LAG, chunks)
        def _(j):
            relay(j)

        for step in range(1, nodes):
            hid_copy(step, 2).wait_recv()
            turn(step, 2)

        @pl.loop(0, chunks)
        def _(j):
            product(j, 2)

            @pl.when(j >= FINISH_LAG)
            def _():
                finish(j - FINISH_LAG)

    @pl.loop(chunks - FINISH_LAG, chunks)
    def _(j):
        finish(j)

    for step in range(1, nodes):
        for part in range(len(parts)):
            hid_copy(step, part).wait_send()

    @pl.loop(0, chunks)
    def _(j):
        for step in direct:
            cot_copy(j, step).wait_send()
        if square:
            for way in range(2):
                forward_copy(j, way).wait_send()
        for half in range(len(parts)):
            pair_copy(j, half).wait_send()
        if line:
            mate_copy(j).wait_send()

            @pl.when(edge)
            def _():
                relay_copy(j).wait_send()

            @pl.when(inner)
            def _():
                for k in range(2):
                    cross_copy(j, k).wait_send()
        else:
            for step in range(1, chips):
                z_copy(j, step).wait_send()


def on_device(nodes, replicas, hidden, cotangent, scales):
    tokens, slab = hidden.shape
    width = cotangent.shape[1]
    chunk = 2 * BLOCK
    chunks = width // chunk
    rows = slab // nodes
    final = rows // replicas
    chips = replicas // 2
    slots = 2 if chips == 4 else chips - 1
    bf16 = jnp.bfloat16
    dma = pltpu.SemaphoreType.DMA
    return pl.pallas_call(
        functools.partial(kernel, nodes, replicas, chunk),
        out_shape=jax.ShapeDtypeStruct((final, width), jnp.float32),
        in_specs=[
            pl.BlockSpec(memory_space=pl.ANY),
            pl.BlockSpec(memory_space=pl.ANY),
            pl.BlockSpec(memory_space=pl.ANY),
        ],
        out_specs=pl.BlockSpec(memory_space=pltpu.VMEM),
        scratch_shapes=[
            pltpu.VMEM((tokens, width), bf16),
            pltpu.VMEM((scales.shape[1], rows), jnp.float32),
            pltpu.VMEM((nodes, tokens, rows), bf16),
            pltpu.VMEM((rows, nodes * tokens), bf16),
            pltpu.VMEM((chunks, nodes * tokens, chunk), bf16),
            pltpu.VMEM((chunk, chunk), bf16),
            pltpu.VMEM((BLOCK, rows), jnp.float32),
            pltpu.VMEM((rows, 2 * BLOCK), bf16),
            pltpu.VMEM((rows, 2 * BLOCK), bf16),
            pltpu.VMEM((chunks, rows, chunk), jnp.float32),
            pltpu.VMEM((chunks, 2, chips, final, chunk), bf16),
            pltpu.VMEM((chunks, chips, final, chunk), bf16),
            pltpu.VMEM((chunks, chips, final, chunk), bf16),
            pltpu.VMEM((chunks, slots, final, chunk), bf16),
            pltpu.VMEM((chunks, 2, final, chunk), bf16),
            pltpu.VMEM((chunks, 2, final, chunk), bf16),
            dma((3,)),
            dma((nodes - 1, 3)),
            dma((nodes - 1, 3)),
            dma((chunks, nodes - 1)),
            dma((chunks, nodes - 1)),
            dma((chunks, 3)),
            dma((chunks, 3)),
            dma((chunks, slots)),
            dma((chunks, slots)),
            dma((chunks, 2)),
            dma((chunks, 2)),
            dma((chunks,)),
            dma((chunks,)),
            dma((chunks, 2)),
            dma((chunks,)),
        ],
        compiler_params=pltpu.CompilerParams(
            collective_id=0, has_side_effects=True, vmem_limit_bytes=52 * 1024 * 1024
        ),
        cost_estimate=pl.CostEstimate(
            flops=2 * tokens * slab * width, bytes_accessed=2 * tokens * (slab + width), transcendentals=0
        ),
    )(hidden, cotangent, scales.T)


def solution(mesh):
    in_specs = (P(("node", "replica"), None), P(("node", "replica"), None), P("node", None))
    out_specs = P(("node", "replica"), None)
    return jax.shard_map(
        functools.partial(on_device, mesh.shape["node"], mesh.shape["replica"]),
        mesh=mesh, in_specs=in_specs, out_specs=out_specs, check_vma=False,
    )
```

```python
import functools
import math

import jax
import jax.numpy as jnp
from jax import lax
from jax.experimental import pallas as pl
from jax.experimental.pallas import tpu as pltpu
from jax.sharding import PartitionSpec as P

MESH = pl.DeviceIdType.MESH
BLOCK = 128
WINDOW = 8
AHEAD = 4
LATE_HIDDEN = 6
PAIR_LAG = 1
RELAY_LAG = 4
FINISH_LAG = 8


def kernel(
    nodes, replicas, chunk,
    hidden, cotangent, scales, out,
    raw, scale, hid, hid_t, cot, table, stage, inverse, forward, spread_inverse, levels, partner_in, pair, arrived, relay_in, merged,
    local_sem, hid_send, hid_recv, cot_send, cot_recv, pair_send, pair_recv, z_send, z_recv,
    forward_send, forward_recv, relay_send, relay_recv, cross_send, cross_recv,
):
    chips = replicas // 2
    tokens, slab = hidden.shape
    width = cotangent.shape[1]
    chunks = width // chunk
    rows = slab // nodes
    final = rows // replicas
    tile = 2 * final
    scale_cols = scales.shape[0]
    node = lax.axis_index("node")
    replica = lax.axis_index("replica")
    chip = replica // 2
    core = lax.rem(replica, 2)
    partner = chip * 2 + (1 - core)

    square = nodes == 4
    line = chips == 4
    node_y, node_x = node // 2, lax.rem(node, 2)
    side = chip // 2
    mate = side * 2 + (1 - lax.rem(chip, 2))
    far = 2 * (1 - side)
    inner = lax.rem(chip, 2) == 1 - side
    edge = lax.rem(chip, 2) == side
    direct = (1, 2) if square else tuple(range(1, nodes))
    parts = ((far, 2), (mate, 1), (chip, 1)) if line else ((0, chips),)
    early = parts[:2]

    def peer_node(step):
        if square:
            across_x = 1 - node_x if step % 2 else node_x
            across_y = 1 - node_y if step // 2 else node_y
            return across_y * 2 + across_x
        return lax.rem(node + step, nodes)

    def peer_replica(step):
        return lax.rem(chip + step, chips) * 2 + core

    barrier = pltpu.get_barrier_semaphore()
    for step in range(1, nodes):
        pl.semaphore_signal(barrier, inc=1, device_id={"node": peer_node(step)}, device_id_type=MESH)
    pl.semaphore_signal(barrier, inc=1, device_id={"replica": partner}, device_id_type=MESH)
    for step in range(1, chips):
        pl.semaphore_signal(barrier, inc=1, device_id={"replica": peer_replica(step)}, device_id_type=MESH)

    def own_hidden():
        begin = pl.multiple_of(node * rows, BLOCK)
        return pltpu.make_async_copy(hidden.at[:, pl.ds(begin, rows)], hid.at[0], local_sem.at[0])

    def own_cot():
        return pltpu.make_async_copy(cotangent, raw, local_sem.at[1])

    def slot(step):
        return slice(step * tokens, (step + 1) * tokens)

    def hid_copy(step, part):
        to = peer_node(step)
        first, count = parts[part]
        source = pl.multiple_of(to * rows + first * tile, BLOCK)
        target = pl.multiple_of(first * tile, BLOCK)
        return pltpu.make_async_remote_copy(
            hidden.at[:, pl.ds(source, count * tile)], hid.at[step, :, pl.ds(target, count * tile)],
            hid_send.at[step - 1, part], hid_recv.at[step - 1, part],
            device_id={"node": to}, device_id_type=MESH,
        )

    def send_hid(part):
        for step in reversed(range(1, nodes)):
            hid_copy(step, part).start()

    def cot_copy(j, step):
        return pltpu.make_async_remote_copy(
            cot.at[j, slot(0)], cot.at[j, slot(step)],
            cot_send.at[j, step - 1], cot_recv.at[j, step - 1],
            device_id={"node": peer_node(step)}, device_id_type=MESH,
        )

    def forward_copy(j, way):
        part = tokens // 2
        return pltpu.make_async_remote_copy(
            cot.at[j, pl.ds((1 + way) * tokens + way * part, part)],
            cot.at[j, pl.ds(3 * tokens + way * part, part)], forward_send.at[j, way], forward_recv.at[j, way],
            device_id={"node": peer_node(2 - way)}, device_id_type=MESH,
        )

    def pass_on(j):
        for way in range(2):
            cot_copy(j, 1 + way).wait_recv()
            forward_copy(j, way).start()

    def pair_copy(j, half):
        first, count = parts[half]
        return pltpu.make_async_remote_copy(
            levels.at[j, 1 - core, pl.ds(first, count)], partner_in.at[j, pl.ds(first, count)],
            pair_send.at[j, half], pair_recv.at[j, half],
            device_id={"replica": partner}, device_id_type=MESH,
        )

    def mate_copy(j):
        return pltpu.make_async_remote_copy(
            pair.at[j, mate], arrived.at[j, 0], z_send.at[j, 0], z_recv.at[j, 0],
            device_id={"replica": mate * 2 + core}, device_id_type=MESH,
        )

    def relay_copy(j):
        return pltpu.make_async_remote_copy(
            pair.at[j, pl.ds(far, 2)], relay_in.at[j], relay_send.at[j], relay_recv.at[j],
            device_id={"replica": mate * 2 + core}, device_id_type=MESH,
        )

    def cross_copy(j, k):
        return pltpu.make_async_remote_copy(
            merged.at[j, k], arrived.at[j, 1], cross_send.at[j, k], cross_recv.at[j],
            device_id={"replica": (far + k) * 2 + core}, device_id_type=MESH,
        )

    def relay(j):
        @pl.when(inner)
        def _():
            relay_copy(j).wait_recv()
            for k in range(2):
                both = pair[j, far + k].astype(jnp.float32) + relay_in[j, k].astype(jnp.float32)
                merged[j, k] = both.astype(jnp.bfloat16)
                cross_copy(j, k).start()

    def z_copy(j, step):
        to = lax.rem(chip + step, chips)
        return pltpu.make_async_remote_copy(
            pair.at[j, to], arrived.at[j, step - 1], z_send.at[j, step - 1], z_recv.at[j, step - 1],
            device_id={"replica": to * 2 + core}, device_id_type=MESH,
        )

    own_hidden().start()

    own_cot().start()
    own_scales = pltpu.make_async_copy(scales, scale, local_sem.at[2])
    own_scales.start()

    pl.semaphore_wait(barrier, nodes - 1 + chips)
    for part in range(len(early)):
        send_hid(part)

    def send_cot(j):
        for step in direct:
            cot_copy(j, step).start()

    row_index = lax.broadcasted_iota(jnp.int32, (chunk, chunk), 0)
    col_index = lax.broadcasted_iota(jnp.int32, (chunk, chunk), 1)
    bits = jnp.bitwise_and(jnp.bitwise_and(row_index, col_index), BLOCK - 1)
    for shift in (4, 2, 1):
        bits = jnp.bitwise_xor(bits, jnp.right_shift(bits, shift))
    signs = 1.0 - 2.0 * jnp.bitwise_and(bits, 1).astype(jnp.float32)
    same = jnp.right_shift(row_index, 7) == jnp.right_shift(col_index, 7)
    table[...] = jnp.where(same, signs, 0.0).astype(jnp.bfloat16)

    def spread(j):
        source = lax.broadcasted_iota(jnp.int32, (2 * BLOCK, chunk), 0)
        target = lax.broadcasted_iota(jnp.int32, (2 * BLOCK, chunk), 1)
        hit = jnp.bitwise_and(source, BLOCK - 1) == jnp.right_shift(target, 7) + j * (chunk // BLOCK)
        return jnp.where(hit, 1.0, 0.0).astype(jnp.bfloat16)

    def mul(left, right):
        return jnp.dot(left, right, preferred_element_type=jnp.float32)

    def rotate(value):
        high = value.astype(jnp.bfloat16)
        low = (value - high.astype(jnp.float32)).astype(jnp.bfloat16)
        return mul(high, table[...]) + mul(low, table[...])

    own_cot().wait()

    @pl.loop(0, chunks)
    def _(j):
        block = raw[:, pl.ds(pl.multiple_of(j * chunk, BLOCK), chunk)]
        cot[j, slot(0)] = mul(block, table[...]).astype(jnp.bfloat16)

    def split_store(ref, value):
        stage[...] = jnp.zeros_like(stage)
        stage[:scale_cols, :] = value
        for part in range(rows // BLOCK):
            span = slice(part * BLOCK, (part + 1) * BLOCK)
            turned = stage[:, span].T
            high = turned.astype(jnp.bfloat16)
            ref[span, :BLOCK] = high
            ref[span, BLOCK:] = (turned - high.astype(jnp.float32)).astype(jnp.bfloat16)

    norm = 1.0 / math.sqrt(BLOCK)
    own_scales.wait()
    split_store(inverse, norm / scale[...])
    split_store(forward, norm * scale[...])

    @pl.loop(0, chunks)
    def _(j):
        spread_inverse[j] = mul(inverse[...], spread(j))

    def turn(step, part):
        first, count = parts[part]
        for piece in range(count * tile // BLOCK):
            span = pl.ds(pl.multiple_of(first * tile + piece * BLOCK, BLOCK), BLOCK)
            hid_t[span, slot(step)] = hid[step, :, span].T

    own_hidden().wait()
    for part in range(len(parts)):
        turn(0, part)
    for part in range(len(early)):
        for step in direct:
            hid_copy(step, part).wait_recv()
    for j in range(AHEAD):
        send_cot(j)
    for part in range(len(early)):
        for step in direct:
            turn(step, part)
    if square:
        for part in range(len(early)):
            hid_copy(3, part).wait_recv()
        for j in range(AHEAD):
            pass_on(j)
            send_cot(j + AHEAD)
        for part in range(len(early)):
            turn(3, part)
    else:
        for j in range(AHEAD, WINDOW):
            send_cot(j)

    own_rows = pl.ds(pl.multiple_of(replica * final, final), final)

    def finish(j):
        if line:
            pair_copy(j, 2).wait_recv()
            mate_copy(j).wait_recv()
            cross_copy(j, 0).wait_recv()
            total = levels[j, core, chip].astype(jnp.float32) + partner_in[j, chip].astype(jnp.float32)
        else:
            total = pair[j, chip].astype(jnp.float32)
        for k in range(arrived.shape[1]):
            if not line:
                z_copy(j, k + 1).wait_recv()
            total = total + arrived[j, k].astype(jnp.float32)
        total = total * mul(forward[own_rows, :], spread(j))
        out[:, pl.ds(pl.multiple_of(j * chunk, BLOCK), chunk)] = rotate(total)

    def product(j, part):
        first, count = parts[part]
        span = pl.ds(pl.multiple_of(first * tile, tile), count * tile)
        level = mul(hid_t[span, :], cot[j]) * spread_inverse[j, span]
        level = jnp.clip(level, -7.0, 7.0).astype(jnp.bfloat16)
        for z in range(count):
            levels[j, 0, first + z] = level[z * tile:z * tile + final]
            levels[j, 1, first + z] = level[z * tile + final:(z + 1) * tile]
        pair_copy(j, part).start()

    def combine(j):
        for part, (first, count) in enumerate(early):
            pair_copy(j, part).wait_recv()
            for z in range(count):
                both = levels[j, core, first + z].astype(jnp.float32) + partner_in[j, first + z].astype(jnp.float32)
                pair[j, first + z] = both.astype(jnp.bfloat16)

            if line and part == 0:
                @pl.when(edge)
                def _():
                    relay_copy(j).start()

        if line:
            mate_copy(j).start()
        else:
            for step in range(1, chips):
                z_copy(j, step).start()

    @pl.loop(0, chunks)
    def _(j):
        if square:
            @pl.when(j + AHEAD < chunks)
            def _():
                pass_on(j + AHEAD)

        @pl.when(j + WINDOW < chunks)
        def _():
            send_cot(j + WINDOW)

        if square:
            for way in range(2):
                forward_copy(j, way).wait_recv()
        else:
            for step in direct:
                cot_copy(j, step).wait_recv()

        if line:
            @pl.when(j == chunks - LATE_HIDDEN)
            def _():
                send_hid(2)

        for part in range(len(early)):
            product(j, part)

        @pl.when(j >= PAIR_LAG)
        def _():
            combine(j - PAIR_LAG)

        if line:
            @pl.when(j >= RELAY_LAG)
            def _():
                relay(j - RELAY_LAG)
        else:
            @pl.when(j >= FINISH_LAG)
            def _():
                finish(j - FINISH_LAG)

    for j in range(chunks - PAIR_LAG, chunks):
        combine(j)

    if line:
        @pl.loop(chunks - RELAY_LAG, chunks)
        def _(j):
            relay(j)

        for step in range(1, nodes):
            hid_copy(step, 2).wait_recv()
            turn(step, 2)

        @pl.loop(0, chunks)
        def _(j):
            product(j, 2)

            @pl.when(j >= FINISH_LAG)
            def _():
                finish(j - FINISH_LAG)

    @pl.loop(chunks - FINISH_LAG, chunks)
    def _(j):
        finish(j)

    for step in range(1, nodes):
        for part in range(len(parts)):
            hid_copy(step, part).wait_send()

    @pl.loop(0, chunks)
    def _(j):
        for step in direct:
            cot_copy(j, step).wait_send()
        if square:
            for way in range(2):
                forward_copy(j, way).wait_send()
        for half in range(len(parts)):
            pair_copy(j, half).wait_send()
        if line:
            mate_copy(j).wait_send()

            @pl.when(edge)
            def _():
                relay_copy(j).wait_send()

            @pl.when(inner)
            def _():
                for k in range(2):
                    cross_copy(j, k).wait_send()
        else:
            for step in range(1, chips):
                z_copy(j, step).wait_send()


def on_device(nodes, replicas, hidden, cotangent, scales):
    tokens, slab = hidden.shape
    width = cotangent.shape[1]
    chunk = BLOCK
    chunks = width // chunk
    rows = slab // nodes
    final = rows // replicas
    chips = replicas // 2
    slots = 2 if chips == 4 else chips - 1
    bf16 = jnp.bfloat16
    dma = pltpu.SemaphoreType.DMA
    return pl.pallas_call(
        functools.partial(kernel, nodes, replicas, chunk),
        out_shape=jax.ShapeDtypeStruct((final, width), jnp.float32),
        in_specs=[
            pl.BlockSpec(memory_space=pl.ANY),
            pl.BlockSpec(memory_space=pl.ANY),
            pl.BlockSpec(memory_space=pl.ANY),
        ],
        out_specs=pl.BlockSpec(memory_space=pltpu.VMEM),
        scratch_shapes=[
            pltpu.VMEM((tokens, width), bf16),
            pltpu.VMEM((scales.shape[1], rows), jnp.float32),
            pltpu.VMEM((nodes, tokens, rows), bf16),
            pltpu.VMEM((rows, nodes * tokens), bf16),
            pltpu.VMEM((chunks, nodes * tokens, chunk), bf16),
            pltpu.VMEM((chunk, chunk), bf16),
            pltpu.VMEM((BLOCK, rows), jnp.float32),
            pltpu.VMEM((rows, 2 * BLOCK), bf16),
            pltpu.VMEM((rows, 2 * BLOCK), bf16),
            pltpu.VMEM((chunks, rows, chunk), jnp.float32),
            pltpu.VMEM((chunks, 2, chips, final, chunk), bf16),
            pltpu.VMEM((chunks, chips, final, chunk), bf16),
            pltpu.VMEM((chunks, chips, final, chunk), bf16),
            pltpu.VMEM((chunks, slots, final, chunk), bf16),
            pltpu.VMEM((chunks, 2, final, chunk), bf16),
            pltpu.VMEM((chunks, 2, final, chunk), bf16),
            dma((3,)),
            dma((nodes - 1, 3)),
            dma((nodes - 1, 3)),
            dma((chunks, nodes - 1)),
            dma((chunks, nodes - 1)),
            dma((chunks, 3)),
            dma((chunks, 3)),
            dma((chunks, slots)),
            dma((chunks, slots)),
            dma((chunks, 2)),
            dma((chunks, 2)),
            dma((chunks,)),
            dma((chunks,)),
            dma((chunks, 2)),
            dma((chunks,)),
        ],
        compiler_params=pltpu.CompilerParams(
            collective_id=0, has_side_effects=True, vmem_limit_bytes=52 * 1024 * 1024
        ),
        cost_estimate=pl.CostEstimate(
            flops=2 * tokens * slab * width, bytes_accessed=2 * tokens * (slab + width), transcendentals=0
        ),
    )(hidden, cotangent, scales.T)


def solution(mesh):
    in_specs = (P(("node", "replica"), None), P(("node", "replica"), None), P("node", None))
    out_specs = P(("node", "replica"), None)
    return jax.shard_map(
        functools.partial(on_device, mesh.shape["node"], mesh.shape["replica"]),
        mesh=mesh, in_specs=in_specs, out_specs=out_specs, check_vma=False,
    )
```

```python
import functools
import math

import jax
import jax.numpy as jnp
from jax import lax
from jax.experimental import pallas as pl
from jax.experimental.pallas import tpu as pltpu
from jax.sharding import PartitionSpec as P

MESH = pl.DeviceIdType.MESH
BLOCK = 128
WINDOW = 4
AHEAD = 2
LATE_HIDDEN = 3
RELAY_LAG = 2
LAST = 2


def kernel(
    nodes, replicas, chunk,
    hidden, cotangent, scales, out,
    raw, scale, hid, hid_t, cot, table, stage, inverse, forward, spread_inverse, spread_forward, levels, partner_in, pair, arrived, relay_in, merged,
    local_sem, hid_send, hid_recv, cot_send, cot_recv, pair_send, pair_recv, z_send, z_recv,
    forward_send, forward_recv, relay_send, relay_recv, cross_send, cross_recv,
):
    chips = replicas // 2
    tokens, slab = hidden.shape
    width = cotangent.shape[1]
    chunks = width // chunk
    rows = slab // nodes
    final = rows // replicas
    tile = 2 * final
    scale_cols = scales.shape[0]
    node = lax.axis_index("node")
    replica = lax.axis_index("replica")
    chip = replica // 2
    core = lax.rem(replica, 2)
    partner = chip * 2 + (1 - core)

    square = nodes == 4
    line = chips == 4
    node_y, node_x = node // 2, lax.rem(node, 2)
    side = chip // 2
    mate = side * 2 + (1 - lax.rem(chip, 2))
    far = 2 * (1 - side)
    inner = lax.rem(chip, 2) == 1 - side
    edge = lax.rem(chip, 2) == side
    direct = (1, 2) if square else tuple(range(1, nodes))
    parts = ((far, 2), (mate, 1), (chip, 1)) if line else ((0, chips),)
    early = parts[:2]

    def peer_node(step):
        if square:
            across_x = 1 - node_x if step % 2 else node_x
            across_y = 1 - node_y if step // 2 else node_y
            return across_y * 2 + across_x
        return lax.rem(node + step, nodes)

    def peer_replica(step):
        return lax.rem(chip + step, chips) * 2 + core

    barrier = pltpu.get_barrier_semaphore()
    for step in range(1, nodes):
        pl.semaphore_signal(barrier, inc=1, device_id={"node": peer_node(step)}, device_id_type=MESH)
    pl.semaphore_signal(barrier, inc=1, device_id={"replica": partner}, device_id_type=MESH)
    for step in range(1, chips):
        pl.semaphore_signal(barrier, inc=1, device_id={"replica": peer_replica(step)}, device_id_type=MESH)

    def own_hidden():
        begin = pl.multiple_of(node * rows, BLOCK)
        return pltpu.make_async_copy(hidden.at[:, pl.ds(begin, rows)], hid.at[0], local_sem.at[0])

    def own_cot():
        return pltpu.make_async_copy(cotangent, raw, local_sem.at[1])

    def slot(step):
        return slice(step * tokens, (step + 1) * tokens)

    def hid_copy(step, part):
        to = peer_node(step)
        first, count = parts[part]
        source = pl.multiple_of(to * rows + first * tile, BLOCK)
        target = pl.multiple_of(first * tile, BLOCK)
        return pltpu.make_async_remote_copy(
            hidden.at[:, pl.ds(source, count * tile)], hid.at[step, :, pl.ds(target, count * tile)],
            hid_send.at[step - 1, part], hid_recv.at[step - 1, part],
            device_id={"node": to}, device_id_type=MESH,
        )

    def send_hid(part):
        for step in reversed(range(1, nodes)):
            hid_copy(step, part).start()

    def cot_copy(j, step):
        return pltpu.make_async_remote_copy(
            cot.at[j, slot(0)], cot.at[j, slot(step)],
            cot_send.at[j, step - 1], cot_recv.at[j, step - 1],
            device_id={"node": peer_node(step)}, device_id_type=MESH,
        )

    def forward_copy(j, way):
        part = tokens // 2
        return pltpu.make_async_remote_copy(
            cot.at[j, pl.ds((1 + way) * tokens + way * part, part)],
            cot.at[j, pl.ds(3 * tokens + way * part, part)], forward_send.at[j, way], forward_recv.at[j, way],
            device_id={"node": peer_node(2 - way)}, device_id_type=MESH,
        )

    def pass_on(j):
        for way in range(2):
            cot_copy(j, 1 + way).wait_recv()
            forward_copy(j, way).start()

    def pair_copy(j, half):
        first, count = parts[half]
        return pltpu.make_async_remote_copy(
            levels.at[j, 1 - core, pl.ds(first, count)], partner_in.at[j, pl.ds(first, count)],
            pair_send.at[j, half], pair_recv.at[j, half],
            device_id={"replica": partner}, device_id_type=MESH,
        )

    def mate_copy(j):
        return pltpu.make_async_remote_copy(
            pair.at[j, mate], arrived.at[j, 0], z_send.at[j, 0], z_recv.at[j, 0],
            device_id={"replica": mate * 2 + core}, device_id_type=MESH,
        )

    def relay_copy(j):
        return pltpu.make_async_remote_copy(
            pair.at[j, pl.ds(far, 2)], relay_in.at[j], relay_send.at[j], relay_recv.at[j],
            device_id={"replica": mate * 2 + core}, device_id_type=MESH,
        )

    def cross_copy(j, k):
        return pltpu.make_async_remote_copy(
            merged.at[j, k], arrived.at[j, 1], cross_send.at[j, k], cross_recv.at[j],
            device_id={"replica": (far + k) * 2 + core}, device_id_type=MESH,
        )

    def relay(j):
        @pl.when(inner)
        def _():
            relay_copy(j).wait_recv()
            for k in range(2):
                both = pair[j, far + k].astype(jnp.float32) + relay_in[j, k].astype(jnp.float32)
                merged[j, k] = both.astype(jnp.bfloat16)
                cross_copy(j, k).start()

    def z_copy(j, step):
        to = lax.rem(chip + step, chips)
        return pltpu.make_async_remote_copy(
            pair.at[j, to], arrived.at[j, step - 1], z_send.at[j, step - 1], z_recv.at[j, step - 1],
            device_id={"replica": to * 2 + core}, device_id_type=MESH,
        )

    own_hidden().start()

    own_cot().start()
    own_scales = pltpu.make_async_copy(scales, scale, local_sem.at[2])
    own_scales.start()

    pl.semaphore_wait(barrier, nodes - 1 + chips)
    for part in range(len(early)):
        send_hid(part)

    def send_cot(j):
        for step in direct:
            cot_copy(j, step).start()

    row_index = lax.broadcasted_iota(jnp.int32, (chunk, chunk), 0)
    col_index = lax.broadcasted_iota(jnp.int32, (chunk, chunk), 1)
    bits = jnp.bitwise_and(jnp.bitwise_and(row_index, col_index), BLOCK - 1)
    for shift in (4, 2, 1):
        bits = jnp.bitwise_xor(bits, jnp.right_shift(bits, shift))
    signs = 1.0 - 2.0 * jnp.bitwise_and(bits, 1).astype(jnp.float32)
    same = jnp.right_shift(row_index, 7) == jnp.right_shift(col_index, 7)
    table[...] = jnp.where(same, signs, 0.0).astype(jnp.bfloat16)

    own_rows = pl.ds(pl.multiple_of(replica * final, final), final)

    def spread(j):
        source = lax.broadcasted_iota(jnp.int32, (2 * BLOCK, chunk), 0)
        target = lax.broadcasted_iota(jnp.int32, (2 * BLOCK, chunk), 1)
        hit = jnp.bitwise_and(source, BLOCK - 1) == jnp.right_shift(target, 7) + j * (chunk // BLOCK)
        return jnp.where(hit, 1.0, 0.0).astype(jnp.bfloat16)

    def mul(left, right):
        return jnp.dot(left, right, preferred_element_type=jnp.float32)

    def rotate(value):
        high = value.astype(jnp.bfloat16)
        low = (value - high.astype(jnp.float32)).astype(jnp.bfloat16)
        return mul(high, table[...]) + mul(low, table[...])

    own_cot().wait()

    @pl.loop(0, chunks)
    def _(j):
        block = raw[:, pl.ds(pl.multiple_of(j * chunk, BLOCK), chunk)]
        cot[j, slot(0)] = mul(block, table[...]).astype(jnp.bfloat16)

    send_cot(0)

    def split_store(ref, value):
        stage[...] = jnp.zeros_like(stage)
        stage[:scale_cols, :] = value
        for part in range(rows // BLOCK):
            span = slice(part * BLOCK, (part + 1) * BLOCK)
            turned = stage[:, span].T
            high = turned.astype(jnp.bfloat16)
            ref[span, :BLOCK] = high
            ref[span, BLOCK:] = (turned - high.astype(jnp.float32)).astype(jnp.bfloat16)

    norm = 1.0 / math.sqrt(BLOCK)
    own_scales.wait()
    split_store(inverse, norm / scale[...])
    split_store(forward, norm * scale[...])

    @pl.loop(0, chunks)
    def _(j):
        expand = spread(j)
        spread_inverse[j] = mul(inverse[...], expand)
        spread_forward[j] = mul(forward[own_rows, :], expand)

    def turn(step, part):
        first, count = parts[part]
        for piece in range(count * tile // BLOCK):
            span = pl.ds(pl.multiple_of(first * tile + piece * BLOCK, BLOCK), BLOCK)
            hid_t[span, slot(step)] = hid[step, :, span].T

    own_hidden().wait()
    for part in range(len(parts)):
        turn(0, part)
    for part in range(len(early)):
        for step in direct:
            hid_copy(step, part).wait_recv()
    if square:
        pass_on(0)
    for j in range(1, AHEAD):
        send_cot(j)
    for part in range(len(early)):
        for step in direct:
            turn(step, part)
    if square:
        for part in range(len(early)):
            hid_copy(3, part).wait_recv()
        for j in range(AHEAD):
            send_cot(j + AHEAD)
            if j + 1 < AHEAD:
                pass_on(j + 1)
        for part in range(len(early)):
            turn(3, part)
    else:
        for j in range(AHEAD, WINDOW):
            send_cot(j)

    def await_last(j):
        if line:
            pair_copy(j, 2).wait_recv()
            mate_copy(j).wait_recv()
            cross_copy(j, 0).wait_recv()
        else:
            for step in range(1, chips):
                z_copy(j, step).wait_recv()

    def finish(j):
        if line:
            total = levels[j, core, chip].astype(jnp.float32) + partner_in[j, chip].astype(jnp.float32)
        else:
            total = pair[j, chip].astype(jnp.float32)
        for k in range(arrived.shape[1]):
            total = total + arrived[j, k].astype(jnp.float32)
        total = total * spread_forward[j]
        out[:, pl.ds(pl.multiple_of(j * chunk, BLOCK), chunk)] = rotate(total)

    def product(j, part):
        first, count = parts[part]
        span = pl.ds(pl.multiple_of(first * tile, tile), count * tile)
        level = mul(hid_t[span, :], cot[j]) * spread_inverse[j, span]
        level = jnp.clip(level, -7.0, 7.0).astype(jnp.bfloat16)
        for z in range(count):
            levels[j, 0, first + z] = level[z * tile:z * tile + final]
            levels[j, 1, first + z] = level[z * tile + final:(z + 1) * tile]
        pair_copy(j, part).start()

    def combine(j):
        for part, (first, count) in enumerate(early):
            pair_copy(j, part).wait_recv()
            for z in range(count):
                both = levels[j, core, first + z].astype(jnp.float32) + partner_in[j, first + z].astype(jnp.float32)
                pair[j, first + z] = both.astype(jnp.bfloat16)

            if line and part == 0:
                @pl.when(edge)
                def _():
                    relay_copy(j).start()

        if line:
            mate_copy(j).start()
        else:
            for step in range(1, chips):
                z_copy(j, step).start()

    @pl.loop(0, chunks)
    def _(j):
        if square:
            @pl.when(j + AHEAD < chunks)
            def _():
                pass_on(j + AHEAD)

        @pl.when(j + WINDOW < chunks)
        def _():
            send_cot(j + WINDOW)

        if square:
            for way in range(2):
                forward_copy(j, way).wait_recv()
        else:
            for step in direct:
                cot_copy(j, step).wait_recv()

        if line:
            @pl.when(j == chunks - LATE_HIDDEN)
            def _():
                send_hid(2)

        for part in range(len(early)):
            product(j, part)
        combine(j)

        if line:
            @pl.when(j >= RELAY_LAG)
            def _():
                relay(j - RELAY_LAG)

    if line:
        @pl.loop(chunks - RELAY_LAG, chunks)
        def _(j):
            relay(j)

        for step in range(1, nodes):
            hid_copy(step, 2).wait_recv()
            turn(step, 2)

        for j in range(chunks):
            product(j, 2)

    for group in (range(chunks - LAST), range(chunks - LAST, chunks)):
        for j in group:
            await_last(j)
        for j in group:
            finish(j)

    for step in range(1, nodes):
        for part in range(len(parts)):
            hid_copy(step, part).wait_send()

    @pl.loop(0, chunks)
    def _(j):
        for step in direct:
            cot_copy(j, step).wait_send()
        if square:
            for way in range(2):
                forward_copy(j, way).wait_send()
        for half in range(len(parts)):
            pair_copy(j, half).wait_send()
        if line:
            mate_copy(j).wait_send()

            @pl.when(edge)
            def _():
                relay_copy(j).wait_send()

            @pl.when(inner)
            def _():
                for k in range(2):
                    cross_copy(j, k).wait_send()
        else:
            for step in range(1, chips):
                z_copy(j, step).wait_send()


def on_device(nodes, replicas, hidden, cotangent, scales):
    tokens, slab = hidden.shape
    width = cotangent.shape[1]
    chunk = 2 * BLOCK
    chunks = width // chunk
    rows = slab // nodes
    final = rows // replicas
    chips = replicas // 2
    slots = 2 if chips == 4 else chips - 1
    bf16 = jnp.bfloat16
    dma = pltpu.SemaphoreType.DMA
    return pl.pallas_call(
        functools.partial(kernel, nodes, replicas, chunk),
        out_shape=jax.ShapeDtypeStruct((final, width), jnp.float32),
        in_specs=[
            pl.BlockSpec(memory_space=pl.ANY),
            pl.BlockSpec(memory_space=pl.ANY),
            pl.BlockSpec(memory_space=pl.ANY),
        ],
        out_specs=pl.BlockSpec(memory_space=pltpu.VMEM),
        scratch_shapes=[
            pltpu.VMEM((tokens, width), bf16),
            pltpu.VMEM((scales.shape[1], rows), jnp.float32),
            pltpu.VMEM((nodes, tokens, rows), bf16),
            pltpu.VMEM((rows, nodes * tokens), bf16),
            pltpu.VMEM((chunks, nodes * tokens, chunk), bf16),
            pltpu.VMEM((chunk, chunk), bf16),
            pltpu.VMEM((BLOCK, rows), jnp.float32),
            pltpu.VMEM((rows, 2 * BLOCK), bf16),
            pltpu.VMEM((rows, 2 * BLOCK), bf16),
            pltpu.VMEM((chunks, rows, chunk), jnp.float32),
            pltpu.VMEM((chunks, final, chunk), jnp.float32),
            pltpu.VMEM((chunks, 2, chips, final, chunk), bf16),
            pltpu.VMEM((chunks, chips, final, chunk), bf16),
            pltpu.VMEM((chunks, chips, final, chunk), bf16),
            pltpu.VMEM((chunks, slots, final, chunk), bf16),
            pltpu.VMEM((chunks, 2, final, chunk), bf16),
            pltpu.VMEM((chunks, 2, final, chunk), bf16),
            dma((3,)),
            dma((nodes - 1, 3)),
            dma((nodes - 1, 3)),
            dma((chunks, nodes - 1)),
            dma((chunks, nodes - 1)),
            dma((chunks, 3)),
            dma((chunks, 3)),
            dma((chunks, slots)),
            dma((chunks, slots)),
            dma((chunks, 2)),
            dma((chunks, 2)),
            dma((chunks,)),
            dma((chunks,)),
            dma((chunks, 2)),
            dma((chunks,)),
        ],
        compiler_params=pltpu.CompilerParams(
            collective_id=0, has_side_effects=True, vmem_limit_bytes=52 * 1024 * 1024
        ),
        cost_estimate=pl.CostEstimate(
            flops=2 * tokens * slab * width, bytes_accessed=2 * tokens * (slab + width), transcendentals=0
        ),
    )(hidden, cotangent, scales.T)


def solution(mesh):
    in_specs = (P(("node", "replica"), None), P(("node", "replica"), None), P("node", None))
    out_specs = P(("node", "replica"), None)
    return jax.shard_map(
        functools.partial(on_device, mesh.shape["node"], mesh.shape["replica"]),
        mesh=mesh, in_specs=in_specs, out_specs=out_specs, check_vma=False,
    )
```

```python
import functools
import math

import jax
import jax.numpy as jnp
from jax import lax
from jax.experimental import pallas as pl
from jax.experimental.pallas import tpu as pltpu
from jax.sharding import PartitionSpec as P

MESH = pl.DeviceIdType.MESH
BLOCK = 128
WINDOW = 5
AHEAD = 2
LATE_HIDDEN = 3
RELAY_LAG = 3
LAST = 2


def kernel(
    nodes, replicas, chunk,
    hidden, cotangent, scales, out,
    raw, scale, hid, hid_t, cot, table, stage, inverse, forward, spread_inverse, spread_forward, levels, partner_in, pair, arrived, relay_in, merged,
    local_sem, hid_send, hid_recv, cot_send, cot_recv, pair_send, pair_recv, z_send, z_recv,
    forward_send, forward_recv, relay_send, relay_recv, cross_send, cross_recv,
):
    chips = replicas // 2
    tokens, slab = hidden.shape
    width = cotangent.shape[1]
    chunks = width // chunk
    rows = slab // nodes
    final = rows // replicas
    tile = 2 * final
    scale_cols = scales.shape[0]
    node = lax.axis_index("node")
    replica = lax.axis_index("replica")
    chip = replica // 2
    core = lax.rem(replica, 2)
    partner = chip * 2 + (1 - core)

    square = nodes == 4
    line = chips == 4
    node_y, node_x = node // 2, lax.rem(node, 2)
    side = chip // 2
    mate = side * 2 + (1 - lax.rem(chip, 2))
    far = 2 * (1 - side)
    inner = lax.rem(chip, 2) == 1 - side
    edge = lax.rem(chip, 2) == side
    direct = (1, 2) if square else tuple(range(1, nodes))
    parts = ((far, 2), (mate, 1), (chip, 1)) if line else ((0, chips),)
    early = parts[:2]

    def peer_node(step):
        if square:
            across_x = 1 - node_x if step % 2 else node_x
            across_y = 1 - node_y if step // 2 else node_y
            return across_y * 2 + across_x
        return lax.rem(node + step, nodes)

    def peer_replica(step):
        return lax.rem(chip + step, chips) * 2 + core

    barrier = pltpu.get_barrier_semaphore()
    for step in range(1, nodes):
        pl.semaphore_signal(barrier, inc=1, device_id={"node": peer_node(step)}, device_id_type=MESH)
    pl.semaphore_signal(barrier, inc=1, device_id={"replica": partner}, device_id_type=MESH)
    for step in range(1, chips):
        pl.semaphore_signal(barrier, inc=1, device_id={"replica": peer_replica(step)}, device_id_type=MESH)

    def own_hidden():
        begin = pl.multiple_of(node * rows, BLOCK)
        return pltpu.make_async_copy(hidden.at[:, pl.ds(begin, rows)], hid.at[0], local_sem.at[0])

    def own_cot():
        return pltpu.make_async_copy(cotangent, raw, local_sem.at[1])

    def slot(step):
        return slice(step * tokens, (step + 1) * tokens)

    def hid_copy(step, part):
        to = peer_node(step)
        first, count = parts[part]
        source = pl.multiple_of(to * rows + first * tile, BLOCK)
        target = pl.multiple_of(first * tile, BLOCK)
        return pltpu.make_async_remote_copy(
            hidden.at[:, pl.ds(source, count * tile)], hid.at[step, :, pl.ds(target, count * tile)],
            hid_send.at[step - 1, part], hid_recv.at[step - 1, part],
            device_id={"node": to}, device_id_type=MESH,
        )

    def send_hid(part):
        for step in reversed(range(1, nodes)):
            hid_copy(step, part).start()

    def cot_copy(j, step):
        return pltpu.make_async_remote_copy(
            cot.at[j, slot(0)], cot.at[j, slot(step)],
            cot_send.at[j, step - 1], cot_recv.at[j, step - 1],
            device_id={"node": peer_node(step)}, device_id_type=MESH,
        )

    def forward_copy(j, way):
        part = tokens // 2
        return pltpu.make_async_remote_copy(
            cot.at[j, pl.ds((1 + way) * tokens + way * part, part)],
            cot.at[j, pl.ds(3 * tokens + way * part, part)], forward_send.at[j, way], forward_recv.at[j, way],
            device_id={"node": peer_node(2 - way)}, device_id_type=MESH,
        )

    def pass_on(j):
        for way in range(2):
            cot_copy(j, 1 + way).wait_recv()
            forward_copy(j, way).start()

    def pair_copy(j, half):
        first, count = parts[half]
        return pltpu.make_async_remote_copy(
            levels.at[j, 1 - core, pl.ds(first, count)], partner_in.at[j, pl.ds(first, count)],
            pair_send.at[j, half], pair_recv.at[j, half],
            device_id={"replica": partner}, device_id_type=MESH,
        )

    def mate_copy(j):
        return pltpu.make_async_remote_copy(
            pair.at[j, mate], arrived.at[j, 0], z_send.at[j, 0], z_recv.at[j, 0],
            device_id={"replica": mate * 2 + core}, device_id_type=MESH,
        )

    def relay_copy(j):
        return pltpu.make_async_remote_copy(
            pair.at[j, pl.ds(far, 2)], relay_in.at[j], relay_send.at[j], relay_recv.at[j],
            device_id={"replica": mate * 2 + core}, device_id_type=MESH,
        )

    def cross_copy(j, k):
        return pltpu.make_async_remote_copy(
            merged.at[j, k], arrived.at[j, 1], cross_send.at[j, k], cross_recv.at[j],
            device_id={"replica": (far + k) * 2 + core}, device_id_type=MESH,
        )

    def relay(j):
        @pl.when(inner)
        def _():
            relay_copy(j).wait_recv()
            for k in range(2):
                both = pair[j, far + k].astype(jnp.float32) + relay_in[j, k].astype(jnp.float32)
                merged[j, k] = both.astype(jnp.bfloat16)
                cross_copy(j, k).start()

    def z_copy(j, step):
        to = lax.rem(chip + step, chips)
        return pltpu.make_async_remote_copy(
            pair.at[j, to], arrived.at[j, step - 1], z_send.at[j, step - 1], z_recv.at[j, step - 1],
            device_id={"replica": to * 2 + core}, device_id_type=MESH,
        )

    own_hidden().start()

    own_cot().start()
    own_scales = pltpu.make_async_copy(scales, scale, local_sem.at[2])
    own_scales.start()

    pl.semaphore_wait(barrier, nodes - 1 + chips)
    for part in range(len(early)):
        send_hid(part)

    def send_cot(j):
        for step in direct:
            cot_copy(j, step).start()

    row_index = lax.broadcasted_iota(jnp.int32, (chunk, chunk), 0)
    col_index = lax.broadcasted_iota(jnp.int32, (chunk, chunk), 1)
    bits = jnp.bitwise_and(jnp.bitwise_and(row_index, col_index), BLOCK - 1)
    for shift in (4, 2, 1):
        bits = jnp.bitwise_xor(bits, jnp.right_shift(bits, shift))
    signs = 1.0 - 2.0 * jnp.bitwise_and(bits, 1).astype(jnp.float32)
    same = jnp.right_shift(row_index, 7) == jnp.right_shift(col_index, 7)
    table[...] = jnp.where(same, signs, 0.0).astype(jnp.bfloat16)

    own_rows = pl.ds(pl.multiple_of(replica * final, final), final)

    def spread(j):
        source = lax.broadcasted_iota(jnp.int32, (2 * BLOCK, chunk), 0)
        target = lax.broadcasted_iota(jnp.int32, (2 * BLOCK, chunk), 1)
        hit = jnp.bitwise_and(source, BLOCK - 1) == jnp.right_shift(target, 7) + j * (chunk // BLOCK)
        return jnp.where(hit, 1.0, 0.0).astype(jnp.bfloat16)

    def mul(left, right):
        return jnp.dot(left, right, preferred_element_type=jnp.float32)

    def rotate(value):
        high = value.astype(jnp.bfloat16)
        low = (value - high.astype(jnp.float32)).astype(jnp.bfloat16)
        return mul(high, table[...]) + mul(low, table[...])

    own_cot().wait()

    @pl.loop(0, chunks)
    def _(j):
        block = raw[:, pl.ds(pl.multiple_of(j * chunk, BLOCK), chunk)]
        cot[j, slot(0)] = mul(block, table[...]).astype(jnp.bfloat16)

    send_cot(0)

    def split_store(ref, value):
        stage[...] = jnp.zeros_like(stage)
        stage[:scale_cols, :] = value
        for part in range(rows // BLOCK):
            span = slice(part * BLOCK, (part + 1) * BLOCK)
            turned = stage[:, span].T
            high = turned.astype(jnp.bfloat16)
            ref[span, :BLOCK] = high
            ref[span, BLOCK:] = (turned - high.astype(jnp.float32)).astype(jnp.bfloat16)

    norm = 1.0 / math.sqrt(BLOCK)
    own_scales.wait()
    split_store(inverse, norm / scale[...])
    split_store(forward, norm * scale[...])

    @pl.loop(0, chunks)
    def _(j):
        expand = spread(j)
        spread_inverse[j] = mul(inverse[...], expand)
        spread_forward[j] = mul(forward[own_rows, :], expand)

    def turn(step, part):
        first, count = parts[part]
        for piece in range(count * tile // BLOCK):
            span = pl.ds(pl.multiple_of(first * tile + piece * BLOCK, BLOCK), BLOCK)
            hid_t[span, slot(step)] = hid[step, :, span].T

    own_hidden().wait()
    for part in range(len(parts)):
        turn(0, part)
    for part in range(len(early)):
        for step in direct:
            hid_copy(step, part).wait_recv()
    if square:
        pass_on(0)
    for j in range(1, AHEAD):
        send_cot(j)
    for part in range(len(early)):
        for step in direct:
            turn(step, part)
    if square:
        for part in range(len(early)):
            hid_copy(3, part).wait_recv()
        for j in range(1, WINDOW - AHEAD + 1):
            send_cot(j + AHEAD - 1)
            if j < AHEAD:
                pass_on(j)
        for part in range(len(early)):
            turn(3, part)
    else:
        for j in range(AHEAD, WINDOW):
            send_cot(j)

    def await_last(j):
        if line:
            pair_copy(j, 2).wait_recv()
            mate_copy(j).wait_recv()
            cross_copy(j, 0).wait_recv()
        else:
            for step in range(1, chips):
                z_copy(j, step).wait_recv()

    def finish(j):
        if line:
            total = levels[j, core, chip].astype(jnp.float32) + partner_in[j, chip].astype(jnp.float32)
        else:
            total = pair[j, chip].astype(jnp.float32)
        for k in range(arrived.shape[1]):
            total = total + arrived[j, k].astype(jnp.float32)
        total = total * spread_forward[j]
        out[:, pl.ds(pl.multiple_of(j * chunk, BLOCK), chunk)] = rotate(total)

    def product(j, part):
        first, count = parts[part]
        span = pl.ds(pl.multiple_of(first * tile, tile), count * tile)
        level = mul(hid_t[span, :], cot[j]) * spread_inverse[j, span]
        level = jnp.clip(level, -7.0, 7.0).astype(jnp.bfloat16)
        for z in range(count):
            levels[j, 0, first + z] = level[z * tile:z * tile + final]
            levels[j, 1, first + z] = level[z * tile + final:(z + 1) * tile]
        pair_copy(j, part).start()

    def combine(j):
        for part, (first, count) in enumerate(early):
            pair_copy(j, part).wait_recv()
            for z in range(count):
                both = levels[j, core, first + z].astype(jnp.float32) + partner_in[j, first + z].astype(jnp.float32)
                pair[j, first + z] = both.astype(jnp.bfloat16)

            if line and part == 0:
                @pl.when(edge)
                def _():
                    relay_copy(j).start()

        if line:
            mate_copy(j).start()
        else:
            for step in range(1, chips):
                z_copy(j, step).start()

    @pl.loop(0, chunks)
    def _(j):
        if square:
            @pl.when(j + AHEAD < chunks)
            def _():
                pass_on(j + AHEAD)

        @pl.when(j + WINDOW < chunks)
        def _():
            send_cot(j + WINDOW)

        if square:
            for way in range(2):
                forward_copy(j, way).wait_recv()
        else:
            for step in direct:
                cot_copy(j, step).wait_recv()

        if line:
            @pl.when(j == chunks - LATE_HIDDEN)
            def _():
                send_hid(2)

        for part in range(len(early)):
            product(j, part)
        combine(j)

        if line:
            @pl.when(j >= RELAY_LAG)
            def _():
                relay(j - RELAY_LAG)

    if line:
        @pl.loop(chunks - RELAY_LAG, chunks)
        def _(j):
            relay(j)

        for step in range(1, nodes):
            hid_copy(step, 2).wait_recv()
            turn(step, 2)

        for j in range(chunks):
            product(j, 2)

    for group in (range(chunks - LAST), range(chunks - LAST, chunks)):
        for j in group:
            await_last(j)
        for j in group:
            finish(j)

    for step in range(1, nodes):
        for part in range(len(parts)):
            hid_copy(step, part).wait_send()

    @pl.loop(0, chunks)
    def _(j):
        for step in direct:
            cot_copy(j, step).wait_send()
        if square:
            for way in range(2):
                forward_copy(j, way).wait_send()
        for half in range(len(parts)):
            pair_copy(j, half).wait_send()
        if line:
            mate_copy(j).wait_send()

            @pl.when(edge)
            def _():
                relay_copy(j).wait_send()

            @pl.when(inner)
            def _():
                for k in range(2):
                    cross_copy(j, k).wait_send()
        else:
            for step in range(1, chips):
                z_copy(j, step).wait_send()


def on_device(nodes, replicas, hidden, cotangent, scales):
    tokens, slab = hidden.shape
    width = cotangent.shape[1]
    chunk = 2 * BLOCK
    chunks = width // chunk
    rows = slab // nodes
    final = rows // replicas
    chips = replicas // 2
    slots = 2 if chips == 4 else chips - 1
    bf16 = jnp.bfloat16
    dma = pltpu.SemaphoreType.DMA
    return pl.pallas_call(
        functools.partial(kernel, nodes, replicas, chunk),
        out_shape=jax.ShapeDtypeStruct((final, width), jnp.float32),
        in_specs=[
            pl.BlockSpec(memory_space=pl.ANY),
            pl.BlockSpec(memory_space=pl.ANY),
            pl.BlockSpec(memory_space=pl.ANY),
        ],
        out_specs=pl.BlockSpec(memory_space=pltpu.VMEM),
        scratch_shapes=[
            pltpu.VMEM((tokens, width), bf16),
            pltpu.VMEM((scales.shape[1], rows), jnp.float32),
            pltpu.VMEM((nodes, tokens, rows), bf16),
            pltpu.VMEM((rows, nodes * tokens), bf16),
            pltpu.VMEM((chunks, nodes * tokens, chunk), bf16),
            pltpu.VMEM((chunk, chunk), bf16),
            pltpu.VMEM((BLOCK, rows), jnp.float32),
            pltpu.VMEM((rows, 2 * BLOCK), bf16),
            pltpu.VMEM((rows, 2 * BLOCK), bf16),
            pltpu.VMEM((chunks, rows, chunk), jnp.float32),
            pltpu.VMEM((chunks, final, chunk), jnp.float32),
            pltpu.VMEM((chunks, 2, chips, final, chunk), bf16),
            pltpu.VMEM((chunks, chips, final, chunk), bf16),
            pltpu.VMEM((chunks, chips, final, chunk), bf16),
            pltpu.VMEM((chunks, slots, final, chunk), bf16),
            pltpu.VMEM((chunks, 2, final, chunk), bf16),
            pltpu.VMEM((chunks, 2, final, chunk), bf16),
            dma((3,)),
            dma((nodes - 1, 3)),
            dma((nodes - 1, 3)),
            dma((chunks, nodes - 1)),
            dma((chunks, nodes - 1)),
            dma((chunks, 3)),
            dma((chunks, 3)),
            dma((chunks, slots)),
            dma((chunks, slots)),
            dma((chunks, 2)),
            dma((chunks, 2)),
            dma((chunks,)),
            dma((chunks,)),
            dma((chunks, 2)),
            dma((chunks,)),
        ],
        compiler_params=pltpu.CompilerParams(
            collective_id=0, has_side_effects=True, vmem_limit_bytes=52 * 1024 * 1024
        ),
        cost_estimate=pl.CostEstimate(
            flops=2 * tokens * slab * width, bytes_accessed=2 * tokens * (slab + width), transcendentals=0
        ),
    )(hidden, cotangent, scales.T)


def solution(mesh):
    in_specs = (P(("node", "replica"), None), P(("node", "replica"), None), P("node", None))
    out_specs = P(("node", "replica"), None)
    return jax.shard_map(
        functools.partial(on_device, mesh.shape["node"], mesh.shape["replica"]),
        mesh=mesh, in_specs=in_specs, out_specs=out_specs, check_vma=False,
    )
```

```python
import functools
import math

import jax
import jax.numpy as jnp
from jax import lax
from jax.experimental import pallas as pl
from jax.experimental.pallas import tpu as pltpu
from jax.sharding import PartitionSpec as P

MESH = pl.DeviceIdType.MESH
BLOCK = 128
WINDOW = 4
AHEAD = 2
LATE_HIDDEN = 3
RELAY_LAG = 2
LAST = 2


def kernel(
    nodes, replicas, chunk,
    hidden, cotangent, scales, out,
    raw, scale, hid, hid_t, cot, table, stage, inverse, forward, spread_inverse, spread_forward, levels, partner_in, pair, arrived, relay_in, merged,
    local_sem, hid_send, hid_recv, cot_send, cot_recv, pair_send, pair_recv, z_send, z_recv,
    forward_send, forward_recv, relay_send, relay_recv, cross_send, cross_recv,
):
    chips = replicas // 2
    tokens, slab = hidden.shape
    width = cotangent.shape[1]
    chunks = width // chunk
    rows = slab // nodes
    final = rows // replicas
    tile = 2 * final
    scale_cols = scales.shape[0]
    node = lax.axis_index("node")
    replica = lax.axis_index("replica")
    chip = replica // 2
    core = lax.rem(replica, 2)
    partner = chip * 2 + (1 - core)

    square = nodes == 4
    line = chips == 4
    node_y, node_x = node // 2, lax.rem(node, 2)
    side = chip // 2
    mate = side * 2 + (1 - lax.rem(chip, 2))
    far = 2 * (1 - side)
    inner = lax.rem(chip, 2) == 1 - side
    edge = lax.rem(chip, 2) == side
    direct = (1, 2) if square else tuple(range(1, nodes))
    parts = ((far, 2), (mate, 1), (chip, 1)) if line else ((0, chips),)
    early = parts[:2]

    def peer_node(step):
        if square:
            across_x = 1 - node_x if step % 2 else node_x
            across_y = 1 - node_y if step // 2 else node_y
            return across_y * 2 + across_x
        return lax.rem(node + step, nodes)

    def peer_replica(step):
        return lax.rem(chip + step, chips) * 2 + core

    barrier = pltpu.get_barrier_semaphore()
    for step in range(1, nodes):
        pl.semaphore_signal(barrier, inc=1, device_id={"node": peer_node(step)}, device_id_type=MESH)
    pl.semaphore_signal(barrier, inc=1, device_id={"replica": partner}, device_id_type=MESH)
    for step in range(1, chips):
        pl.semaphore_signal(barrier, inc=1, device_id={"replica": peer_replica(step)}, device_id_type=MESH)

    def own_hidden():
        begin = pl.multiple_of(node * rows, BLOCK)
        return pltpu.make_async_copy(hidden.at[:, pl.ds(begin, rows)], hid.at[0], local_sem.at[0])

    def own_cot():
        return pltpu.make_async_copy(cotangent, raw, local_sem.at[1])

    def slot(step):
        return slice(step * tokens, (step + 1) * tokens)

    def hid_copy(step, part):
        to = peer_node(step)
        first, count = parts[part]
        source = pl.multiple_of(to * rows + first * tile, BLOCK)
        target = pl.multiple_of(first * tile, BLOCK)
        return pltpu.make_async_remote_copy(
            hidden.at[:, pl.ds(source, count * tile)], hid.at[step, :, pl.ds(target, count * tile)],
            hid_send.at[step - 1, part], hid_recv.at[step - 1, part],
            device_id={"node": to}, device_id_type=MESH,
        )

    def send_hid(part):
        for step in reversed(range(1, nodes)):
            hid_copy(step, part).start()

    def cot_copy(j, step):
        return pltpu.make_async_remote_copy(
            cot.at[j, slot(0)], cot.at[j, slot(step)],
            cot_send.at[j, step - 1], cot_recv.at[j, step - 1],
            device_id={"node": peer_node(step)}, device_id_type=MESH,
        )

    def forward_copy(j, way):
        part = tokens // 2
        return pltpu.make_async_remote_copy(
            cot.at[j, pl.ds((1 + way) * tokens + way * part, part)],
            cot.at[j, pl.ds(3 * tokens + way * part, part)], forward_send.at[j, way], forward_recv.at[j, way],
            device_id={"node": peer_node(2 - way)}, device_id_type=MESH,
        )

    def pass_on(j):
        for way in range(2):
            cot_copy(j, 1 + way).wait_recv()
            forward_copy(j, way).start()

    def pair_copy(j, half):
        first, count = parts[half]
        return pltpu.make_async_remote_copy(
            levels.at[j, 1 - core, pl.ds(first, count)], partner_in.at[j, pl.ds(first, count)],
            pair_send.at[j, half], pair_recv.at[j, half],
            device_id={"replica": partner}, device_id_type=MESH,
        )

    def mate_copy(j):
        return pltpu.make_async_remote_copy(
            pair.at[j, mate], arrived.at[j, 0], z_send.at[j, 0], z_recv.at[j, 0],
            device_id={"replica": mate * 2 + core}, device_id_type=MESH,
        )

    def relay_copy(j):
        return pltpu.make_async_remote_copy(
            pair.at[j, pl.ds(far, 2)], relay_in.at[j], relay_send.at[j], relay_recv.at[j],
            device_id={"replica": mate * 2 + core}, device_id_type=MESH,
        )

    def cross_copy(j, k):
        return pltpu.make_async_remote_copy(
            merged.at[j, k], arrived.at[j, 1], cross_send.at[j, k], cross_recv.at[j],
            device_id={"replica": (far + k) * 2 + core}, device_id_type=MESH,
        )

    def relay(j):
        @pl.when(inner)
        def _():
            relay_copy(j).wait_recv()
            for k in range(2):
                both = pair[j, far + k].astype(jnp.float32) + relay_in[j, k].astype(jnp.float32)
                merged[j, k] = both.astype(jnp.bfloat16)
                cross_copy(j, k).start()

    def z_copy(j, step):
        to = lax.rem(chip + step, chips)
        return pltpu.make_async_remote_copy(
            pair.at[j, to], arrived.at[j, step - 1], z_send.at[j, step - 1], z_recv.at[j, step - 1],
            device_id={"replica": to * 2 + core}, device_id_type=MESH,
        )

    own_hidden().start()

    own_cot().start()
    own_scales = pltpu.make_async_copy(scales, scale, local_sem.at[2])
    own_scales.start()

    pl.semaphore_wait(barrier, nodes - 1 + chips)
    for part in range(len(early)):
        send_hid(part)

    def send_cot(j):
        for step in direct:
            cot_copy(j, step).start()

    row_index = lax.broadcasted_iota(jnp.int32, (chunk, chunk), 0)
    col_index = lax.broadcasted_iota(jnp.int32, (chunk, chunk), 1)
    bits = jnp.bitwise_and(jnp.bitwise_and(row_index, col_index), BLOCK - 1)
    for shift in (4, 2, 1):
        bits = jnp.bitwise_xor(bits, jnp.right_shift(bits, shift))
    signs = 1.0 - 2.0 * jnp.bitwise_and(bits, 1).astype(jnp.float32)
    same = jnp.right_shift(row_index, 7) == jnp.right_shift(col_index, 7)
    table[...] = jnp.where(same, signs, 0.0).astype(jnp.bfloat16)

    own_rows = pl.ds(pl.multiple_of(replica * final, final), final)

    def spread(j):
        source = lax.broadcasted_iota(jnp.int32, (2 * BLOCK, chunk), 0)
        target = lax.broadcasted_iota(jnp.int32, (2 * BLOCK, chunk), 1)
        hit = jnp.bitwise_and(source, BLOCK - 1) == jnp.right_shift(target, 7) + j * (chunk // BLOCK)
        return jnp.where(hit, 1.0, 0.0).astype(jnp.bfloat16)

    def mul(left, right):
        return jnp.dot(left, right, preferred_element_type=jnp.float32)

    def rotate(value):
        high = value.astype(jnp.bfloat16)
        low = (value - high.astype(jnp.float32)).astype(jnp.bfloat16)
        return mul(high, table[...]) + mul(low, table[...])

    own_cot().wait()

    @pl.loop(0, chunks)
    def _(j):
        block = raw[:, pl.ds(pl.multiple_of(j * chunk, BLOCK), chunk)]
        cot[j, slot(0)] = mul(block, table[...]).astype(jnp.bfloat16)

    send_cot(0)

    def split_store(ref, value):
        stage[...] = jnp.zeros_like(stage)
        stage[:scale_cols, :] = value
        for part in range(rows // BLOCK):
            span = slice(part * BLOCK, (part + 1) * BLOCK)
            turned = stage[:, span].T
            high = turned.astype(jnp.bfloat16)
            ref[span, :BLOCK] = high
            ref[span, BLOCK:] = (turned - high.astype(jnp.float32)).astype(jnp.bfloat16)

    norm = 1.0 / math.sqrt(BLOCK)
    own_scales.wait()
    split_store(inverse, norm / scale[...])
    split_store(forward, norm * scale[...])

    @pl.loop(0, chunks)
    def _(j):
        expand = spread(j)
        spread_inverse[j] = mul(inverse[...], expand)
        spread_forward[j] = mul(forward[own_rows, :], expand)

    def turn(step, part):
        first, count = parts[part]
        for piece in range(count * tile // BLOCK):
            span = pl.ds(pl.multiple_of(first * tile + piece * BLOCK, BLOCK), BLOCK)
            hid_t[span, slot(step)] = hid[step, :, span].T

    own_hidden().wait()
    for part in range(len(parts)):
        turn(0, part)
    for part in range(len(early)):
        for step in direct:
            hid_copy(step, part).wait_recv()
    if square:
        pass_on(0)
    for j in range(1, AHEAD):
        send_cot(j)
    for part in range(len(early)):
        for step in direct:
            turn(step, part)
    if square:
        for part in range(len(early)):
            hid_copy(3, part).wait_recv()
        for j in range(AHEAD):
            send_cot(j + AHEAD)
            if j + 1 < AHEAD:
                pass_on(j + 1)
        for part in range(len(early)):
            turn(3, part)
    else:
        for j in range(AHEAD, WINDOW):
            send_cot(j)

    def await_last(j):
        if line:
            pair_copy(j, 2).wait_recv()
            mate_copy(j).wait_recv()
            cross_copy(j, 0).wait_recv()
        else:
            for step in range(1, chips):
                z_copy(j, step).wait_recv()

    def finish(j):
        if line:
            total = levels[j, core, chip].astype(jnp.float32) + partner_in[j, chip].astype(jnp.float32)
        else:
            total = pair[j, chip].astype(jnp.float32)
        for k in range(arrived.shape[1]):
            total = total + arrived[j, k].astype(jnp.float32)
        total = total * spread_forward[j]
        out[:, pl.ds(pl.multiple_of(j * chunk, BLOCK), chunk)] = rotate(total)

    def product(j, part):
        first, count = parts[part]
        span = pl.ds(pl.multiple_of(first * tile, tile), count * tile)
        level = mul(hid_t[span, :], cot[j]) * spread_inverse[j, span]
        level = jnp.clip(level, -7.0, 7.0).astype(jnp.bfloat16)
        for z in range(count):
            levels[j, 0, first + z] = level[z * tile:z * tile + final]
            levels[j, 1, first + z] = level[z * tile + final:(z + 1) * tile]
        pair_copy(j, part).start()

    def combine(j):
        for part, (first, count) in enumerate(early):
            if line and part == 1:
                @pl.when(j >= RELAY_LAG)
                def _():
                    relay(j - RELAY_LAG)

            pair_copy(j, part).wait_recv()
            for z in range(count):
                both = levels[j, core, first + z].astype(jnp.float32) + partner_in[j, first + z].astype(jnp.float32)
                pair[j, first + z] = both.astype(jnp.bfloat16)

            if line and part == 0:
                @pl.when(edge)
                def _():
                    relay_copy(j).start()

        if line:
            mate_copy(j).start()
        else:
            for step in range(1, chips):
                z_copy(j, step).start()

    @pl.loop(0, chunks)
    def _(j):
        if square:
            @pl.when(j + AHEAD < chunks)
            def _():
                pass_on(j + AHEAD)

        @pl.when(j + WINDOW < chunks)
        def _():
            send_cot(j + WINDOW)

        if square:
            for way in range(2):
                forward_copy(j, way).wait_recv()
        else:
            for step in direct:
                cot_copy(j, step).wait_recv()

        if line:
            @pl.when(j == chunks - LATE_HIDDEN)
            def _():
                send_hid(2)

        for part in range(len(early)):
            product(j, part)
        combine(j)

    if line:
        for j in range(chunks - RELAY_LAG, chunks - 1):
            relay(j)

        for step in range(1, nodes):
            hid_copy(step, 2).wait_recv()
            turn(step, 2)

        for j in range(chunks):
            product(j, 2)

        relay(chunks - 1)

    for group in (range(chunks - LAST), range(chunks - LAST, chunks)):
        for j in group:
            await_last(j)
        for j in group:
            finish(j)

    for step in range(1, nodes):
        for part in range(len(parts)):
            hid_copy(step, part).wait_send()

    @pl.loop(0, chunks)
    def _(j):
        for step in direct:
            cot_copy(j, step).wait_send()
        if square:
            for way in range(2):
                forward_copy(j, way).wait_send()
        for half in range(len(parts)):
            pair_copy(j, half).wait_send()
        if line:
            mate_copy(j).wait_send()

            @pl.when(edge)
            def _():
                relay_copy(j).wait_send()

            @pl.when(inner)
            def _():
                for k in range(2):
                    cross_copy(j, k).wait_send()
        else:
            for step in range(1, chips):
                z_copy(j, step).wait_send()


def on_device(nodes, replicas, hidden, cotangent, scales):
    tokens, slab = hidden.shape
    width = cotangent.shape[1]
    chunk = 2 * BLOCK
    chunks = width // chunk
    rows = slab // nodes
    final = rows // replicas
    chips = replicas // 2
    slots = 2 if chips == 4 else chips - 1
    bf16 = jnp.bfloat16
    dma = pltpu.SemaphoreType.DMA
    return pl.pallas_call(
        functools.partial(kernel, nodes, replicas, chunk),
        out_shape=jax.ShapeDtypeStruct((final, width), jnp.float32),
        in_specs=[
            pl.BlockSpec(memory_space=pl.ANY),
            pl.BlockSpec(memory_space=pl.ANY),
            pl.BlockSpec(memory_space=pl.ANY),
        ],
        out_specs=pl.BlockSpec(memory_space=pltpu.VMEM),
        scratch_shapes=[
            pltpu.VMEM((tokens, width), bf16),
            pltpu.VMEM((scales.shape[1], rows), jnp.float32),
            pltpu.VMEM((nodes, tokens, rows), bf16),
            pltpu.VMEM((rows, nodes * tokens), bf16),
            pltpu.VMEM((chunks, nodes * tokens, chunk), bf16),
            pltpu.VMEM((chunk, chunk), bf16),
            pltpu.VMEM((BLOCK, rows), jnp.float32),
            pltpu.VMEM((rows, 2 * BLOCK), bf16),
            pltpu.VMEM((rows, 2 * BLOCK), bf16),
            pltpu.VMEM((chunks, rows, chunk), jnp.float32),
            pltpu.VMEM((chunks, final, chunk), jnp.float32),
            pltpu.VMEM((chunks, 2, chips, final, chunk), bf16),
            pltpu.VMEM((chunks, chips, final, chunk), bf16),
            pltpu.VMEM((chunks, chips, final, chunk), bf16),
            pltpu.VMEM((chunks, slots, final, chunk), bf16),
            pltpu.VMEM((chunks, 2, final, chunk), bf16),
            pltpu.VMEM((chunks, 2, final, chunk), bf16),
            dma((3,)),
            dma((nodes - 1, 3)),
            dma((nodes - 1, 3)),
            dma((chunks, nodes - 1)),
            dma((chunks, nodes - 1)),
            dma((chunks, 3)),
            dma((chunks, 3)),
            dma((chunks, slots)),
            dma((chunks, slots)),
            dma((chunks, 2)),
            dma((chunks, 2)),
            dma((chunks,)),
            dma((chunks,)),
            dma((chunks, 2)),
            dma((chunks,)),
        ],
        compiler_params=pltpu.CompilerParams(
            collective_id=0, has_side_effects=True, vmem_limit_bytes=52 * 1024 * 1024
        ),
        cost_estimate=pl.CostEstimate(
            flops=2 * tokens * slab * width, bytes_accessed=2 * tokens * (slab + width), transcendentals=0
        ),
    )(hidden, cotangent, scales.T)


def solution(mesh):
    in_specs = (P(("node", "replica"), None), P(("node", "replica"), None), P("node", None))
    out_specs = P(("node", "replica"), None)
    return jax.shard_map(
        functools.partial(on_device, mesh.shape["node"], mesh.shape["replica"]),
        mesh=mesh, in_specs=in_specs, out_specs=out_specs, check_vma=False,
    )
```
